32 devices in a mesh: ctx: 4 (over z), exp: 8 (over y, x, core).
Axes of the slice: x: 2, y: 2, z: 4, core: 2. Of those that a mesh axis runs over, the one named last changes fastest.
Arguments:
- q_nope: bfloat16 [1024, 16384], P('ctx', 'exp'), may hold values from -6 to 6
- q_rope: bfloat16 [1024, 8192], P('ctx', 'exp'), may hold values from -24 to 24
- kv_latent: bfloat16 [1024, 512], P('ctx'), may hold values from -6 to 6
- key_rope: bfloat16 [1024, 64], P('ctx'), may hold values from -6 to 6
- w_uk: bfloat16 [128, 128, 512], P('exp'), may hold values from -0.5 to 0.5
- w_uv: bfloat16 [128, 512, 128], P('exp'), may hold values from -1 to 1
- w_out: bfloat16 [16384, 7168], P('exp', 'ctx'), may hold values from -0.09375 to 0.09375
- w_gate: bfloat16 [8, 7168, 2048], P('exp', 'ctx'), may hold values from -0.0625 to 0.0625
- w_up: bfloat16 [8, 7168, 2048], P('exp', 'ctx'), may hold values from -0.0625 to 0.0625
- w_down: bfloat16 [8, 2048, 7168], P('exp', None, 'ctx'), may hold values from -0.125 to 0.125
- route_ids: int32 [1024, 4], P('exp'), may hold values from 0 to 7, all different within a row; in each aligned block of 128 rows (0 to 127, 128 to 255, ...) at most 96 rows name the same one
- route_gates: bfloat16 [1024, 4], P('exp'), may hold values from 0.19921875 to 1
Outputs:
- attn_out: bfloat16 [1024, 7168], P('exp', 'ctx')
- moe_out: bfloat16 [1024, 7168], P('exp', 'ctx')
The draws below stay inside these ranges and needn't reach their ends.
Inputs may be any that keep to these rules, and one draw needn't show every extreme that they name: `route_ids`: each row names 4 different experts. In each aligned block of 128 rows no expert is named by more than 96 rows, and in some block one expert is named by exactly 96 rows.
All inputs are finite; a program needn't handle non-finite values.
Results may differ from the reference program's by a relative error of at most 0.035.
Values may be sent and summed in bfloat16 or wider, within the bound.
A program may use at most 128 MiB of HBM per device.

```python
import math
from functools import partial
import jax
import jax.numpy as jnp
import numpy as np
from jax import lax

D = 7168
HEADS = 128
NOPE = 128
ROPE = 64
VHEAD = 128
LATENT = 512
FF = 2048
TOP = 4
SEQ = 1024
ROWS_EXP = 128
EXPERTS = 8
CAP = 96
N_CTX = 4
N_EXP = 8


def draw_q_nope(key, part):
    key = jax.random.fold_in(key, 1)
    return jnp.clip(jax.random.normal(key, (SEQ, HEADS * NOPE), jnp.float32), -6.0, 6.0).astype(jnp.bfloat16)


def draw_key_rope(key, part):
    key = jax.random.fold_in(key, 2)
    values = jnp.clip(jax.random.normal(key, (SEQ, ROPE), jnp.float32), -6.0, 6.0)
    return values.astype(jnp.bfloat16)


def draw_q_rope(key, part):
    key = jax.random.fold_in(key, 3)
    values = jnp.clip(jax.random.normal(key, (SEQ, HEADS * ROPE), jnp.float32), -6.0, 6.0)
    return values.astype(jnp.bfloat16)


def block_scale(own_key, shape, shards, least, top_value):
    def one(axis_at, blocks):
        steps = jax.random.uniform(jax.random.fold_in(jax.random.fold_in(own_key, 6), axis_at), (blocks,), jnp.float32, least / len(shards), top_value / len(shards))
        return jnp.repeat(jnp.exp(steps), shape[axis_at] // blocks).reshape((-1,) + (1,) * (len(shape) - axis_at - 1))

    loudness = one(*shards[0])
    for cut in shards[1:]:
        loudness = loudness * one(*cut)
    return loudness


def assign_block(stream_key, own, number, rows, number_of, top, reach, slope):
    order = jax.random.permutation(stream_key, number_of)
    heavy_load, usual = shares(number_of, rows * top, reach, slope, True), shares(number_of, rows * top, reach, slope, False)
    places = jnp.arange(number_of)

    def named(tallies, turn):
        used = int((tallies > 0).sum())
        fixed = max(1, used // 4)
        moved = fixed + (places - fixed + turn * (used - fixed)) % max(1, number_of - fixed)
        return jnp.zeros((number_of,), jnp.int32).at[order[jnp.where(places < fixed, places, moved)]].set(jnp.asarray(tallies, jnp.int32))

    tallies = jnp.where(number % 4 == 0, named(heavy_load, number // 4), named(usual, number - number // 4 - 1))
    mixed = jax.random.permutation(jax.random.fold_in(own, 3), number_of)
    source_of, receiver = mixed[0:number_of // 2 * 2:2], mixed[1:number_of // 2 * 2:2]
    slack = jnp.minimum(tallies[source_of] - 1, reach - tallies[receiver]) // 2
    slack = jnp.where((source_of == order[0]) | (receiver == order[0]) | (tallies[receiver] == 0), 0, jnp.maximum(slack, 0))
    moved = jax.random.randint(jax.random.fold_in(own, 4), (number_of // 2,), 0, 1 << 20) % (slack + 1)
    tallies = tallies.at[source_of].add(-moved).at[receiver].add(moved)
    labels = jnp.searchsorted(jnp.cumsum(tallies), jnp.arange(rows * top), side="right").astype(jnp.int32)
    listing = labels.reshape(top, rows).T
    listing = listing[jax.random.permutation(jax.random.fold_in(own, 1), rows)]
    turn = jax.random.randint(jax.random.fold_in(own, 2), (rows, 1), 0, top)
    return jnp.take_along_axis(listing, (jnp.arange(top)[None, :] + turn) % top, axis=1)


def shares(count, total, reach, lean, full):
    weights = [(1 << 20) // math.isqrt(standing ** lean) + 1 for standing in range(1, count + 1)]
    largest = reach if full else min(reach, max(-(-total // count), total * weights[0] // sum(weights)))
    least = 1 if total - largest >= count - 1 else 0
    given, surplus = [largest] + [least] * (count - 1), total - largest - least * (count - 1)
    while surplus > 0:
        movable = [i for i in range(1, count) if given[i] < largest] or [i for i in range(1, count) if given[i] < reach]
        mass, budget = sum([weights[i] for i in movable]), surplus
        for i in movable:
            extra = min(reach - given[i], max(1, budget * weights[i] // mass), surplus)
            given[i] = given[i] + extra
            surplus = surplus - extra
    return np.array(given)


def gaussian(stream_key, extent, scale, limit, pieces=(), held_as=jnp.bfloat16):
    level = block_scale(stream_key, extent, pieces, -0.22, 0.18) if pieces else 1.0
    array = jax.random.normal(stream_key, extent, jnp.float32) * scale * level
    return jnp.minimum(jnp.maximum(array, -limit), limit).astype(held_as)


def setup_inputs(seed: int = 0) -> dict:
    arg_keys = jax.random.split(jax.random.key(seed), 13)
    q_nope = draw_q_nope(jax.random.fold_in(arg_keys[12], 71), 0)
    q_rope = draw_q_rope(jax.random.fold_in(arg_keys[12], 71), 0)
    kv_latent = gaussian(arg_keys[2], (SEQ, LATENT), 1.0, 6.0, ((0, 4),))
    key_rope = draw_key_rope(jax.random.fold_in(arg_keys[12], 71), 0)
    w_uk = gaussian(arg_keys[4], (HEADS, NOPE, LATENT), NOPE ** -0.5, 0.5, ((0, 8),))
    w_uv = gaussian(arg_keys[5], (HEADS, LATENT, VHEAD), (LATENT // 16) ** -0.5, 1.0, ((0, 8),))
    w_out = gaussian(arg_keys[6], (HEADS * VHEAD, D), (HEADS * VHEAD // 4) ** -0.5, 0.09375, ((0, 8), (1, 4)))
    w_gate = gaussian(arg_keys[7], (EXPERTS, D, FF), D ** -0.5, 0.0625, ((0, 8), (1, 4)))
    w_up = gaussian(arg_keys[8], (EXPERTS, D, FF), D ** -0.5, 0.0625, ((0, 8), (1, 4)))
    w_down = gaussian(arg_keys[9], (EXPERTS, FF, D), FF ** -0.5, 0.125, ((0, 8), (2, 4)))
    route_ids_keys = jax.random.split(jax.random.fold_in(arg_keys[10], 1), SEQ // ROWS_EXP)
    route_ids_turns = jax.random.permutation(jax.random.fold_in(arg_keys[10], 3), SEQ // ROWS_EXP)
    route_ids = jax.vmap(lambda own, number: assign_block(jax.random.fold_in(arg_keys[10], 2), own, number, ROWS_EXP, EXPERTS, TOP, CAP, 2))(route_ids_keys, route_ids_turns).reshape((SEQ, TOP))
    route_gates = jnp.clip(0.19921875 + 0.80078125 * jax.random.uniform(arg_keys[11], (SEQ, TOP), jnp.float32) ** block_scale(arg_keys[11], (SEQ, TOP), ((0, 8),), -0.2, 0.2), 0.19921875, 1.0).astype(jnp.bfloat16)
    return dict(q_nope=q_nope, q_rope=q_rope, kv_latent=kv_latent, key_rope=key_rope, w_uk=w_uk, w_uv=w_uv, w_out=w_out, w_gate=w_gate, w_up=w_up, w_down=w_down, route_ids=route_ids, route_gates=route_gates)


def head_attention(inputs, kv_latent, key_rope):
    query_nope, query_rope, uk_matrix, uv_matrix = inputs
    query_latent = jnp.dot(query_nope, uk_matrix, preferred_element_type=jnp.float32).astype(jnp.bfloat16)
    scores = jnp.dot(query_latent, kv_latent.T, preferred_element_type=jnp.float32)
    scores = scores + jnp.dot(query_rope, key_rope.T, preferred_element_type=jnp.float32)
    scores = scores * (1.0 / math.sqrt(NOPE + ROPE))
    positions = jnp.arange(SEQ, dtype=jnp.int32)
    allowed = positions[None, :] <= positions[:, None]
    largest = lax.optimization_barrier(jnp.max(jnp.where(allowed, scores, -jnp.inf), axis=1, keepdims=True))
    exp_terms = jnp.where(allowed, jnp.exp(scores - largest), 0.0)
    totals = lax.optimization_barrier(jnp.sum(exp_terms, axis=1, keepdims=True))
    mixed = jnp.dot(exp_terms.astype(jnp.bfloat16), kv_latent, preferred_element_type=jnp.float32)
    latent_out = (mixed / totals).astype(jnp.bfloat16)
    return jnp.dot(latent_out, uv_matrix, preferred_element_type=jnp.float32).astype(jnp.bfloat16)

def expert_rows(inputs, tokens):
    row_index, gate_matrix, up_matrix, down_matrix = inputs
    block_cols = D // N_CTX
    chosen = tokens[row_index].astype(jnp.float32).reshape(-1, N_CTX, block_cols)
    gate_blocks = gate_matrix.astype(jnp.float32).reshape(N_CTX, block_cols, FF)
    up_blocks = up_matrix.astype(jnp.float32).reshape(N_CTX, block_cols, FF)
    gate_part = jnp.einsum('rcd,cdf->crf', chosen, gate_blocks, precision=lax.Precision.HIGHEST).astype(jnp.bfloat16)
    up_part = jnp.einsum('rcd,cdf->crf', chosen, up_blocks, precision=lax.Precision.HIGHEST).astype(jnp.bfloat16)
    gate_pre = lax.optimization_barrier(jnp.sum(gate_part.astype(jnp.float32), axis=0))
    up_pre = lax.optimization_barrier(jnp.sum(up_part.astype(jnp.float32), axis=0))
    hidden = (jax.nn.silu(gate_pre) * up_pre).astype(jnp.bfloat16)
    return jnp.dot(hidden, down_matrix, preferred_element_type=jnp.float32).astype(jnp.bfloat16)

def reference(q_nope, q_rope, kv_latent, key_rope, w_uk, w_uv, w_out, w_gate, w_up, w_down, route_ids, route_gates):
    nope_heads = q_nope.reshape(SEQ, HEADS, NOPE).transpose(1, 0, 2)
    rope_heads = q_rope.reshape(SEQ, HEADS, ROPE).transpose(1, 0, 2)
    head_out = lax.map(partial(head_attention, kv_latent=kv_latent, key_rope=key_rope), (nope_heads, rope_heads, w_uk, w_uv))
    head_flat = head_out.transpose(1, 0, 2).reshape(SEQ, HEADS * VHEAD)
    attn_out = jnp.dot(head_flat, w_out, preferred_element_type=jnp.float32).astype(jnp.bfloat16)
    flat_ids = route_ids.reshape(-1).astype(jnp.int32)
    onehot = (flat_ids[:, None] == jnp.arange(EXPERTS, dtype=jnp.int32)[None, :]).astype(jnp.int32)
    ranks = lax.optimization_barrier(jnp.sum((jnp.cumsum(onehot, axis=0) - onehot) * onehot, axis=1)).astype(jnp.int32)
    owners = jnp.repeat(jnp.arange(SEQ, dtype=jnp.int32), TOP)
    table = jnp.zeros((EXPERTS, N_EXP * CAP), jnp.int32).at[flat_ids, ranks].set(owners)
    outputs = lax.map(partial(expert_rows, tokens=attn_out), (table, w_gate, w_up, w_down))
    picked = outputs[flat_ids, ranks].reshape(SEQ, TOP, D)
    moe_sum = lax.optimization_barrier(jnp.sum(route_gates.astype(jnp.float32)[:, :, None] * picked.astype(jnp.float32), axis=1))
    return (attn_out, moe_sum.astype(jnp.bfloat16))
```

```python
from functools import partial
import math

import jax
import jax.numpy as jnp
from jax import lax
from jax.experimental import pallas as pl
from jax.experimental.pallas import tpu as pltpu
from jax.sharding import PartitionSpec as P

NEG_FILL = -1e30
MESH = pl.DeviceIdType.MESH
CHUNK = 16
BLOCK = 128


def expert_kernel(
    n_ctx, x, wg_hbm, wu_hbm, wd_hbm, out, wg, wu, wd, part, held, hid,
    w_sem, rs_send, rs_recv, ag_send, ag_recv,
):
    p = lax.axis_index("ctx")
    last = n_ctx - 1
    rows = x.shape[0]
    half = rows // 2
    ff = wg.shape[1]
    n = half // CHUNK
    per = BLOCK // CHUNK
    blocks = half // BLOCK
    tile = 512 if ff % 512 == 0 else ff

    loads = [
        pltpu.make_async_copy(src, dst, w_sem.at[i])
        for i, (src, dst) in enumerate(((wg_hbm, wg), (wu_hbm, wu), (wd_hbm, wd)))
    ]
    for load in loads:
        load.start()

    barrier = pltpu.get_barrier_semaphore()

    @pl.when(p > 0)
    def _():
        pl.semaphore_signal(barrier, inc=1, device_id={"ctx": p - 1}, device_id_type=MESH)

    @pl.when(p < last)
    def _():
        pl.semaphore_signal(barrier, inc=1, device_id={"ctx": p + 1}, device_id_type=MESH)

    pl.semaphore_wait(barrier, (p > 0).astype(jnp.int32) + (p < last).astype(jnp.int32))

    ahead = (jnp.minimum(p + 1, last), jnp.maximum(p - 1, 0))

    def chunk_rows(d, t):
        return pl.ds(pl.multiple_of(d * half + t * CHUNK, CHUNK), CHUNK)

    def rs_copy(d, t, src):
        at = chunk_rows(d, t)
        return pltpu.make_async_remote_copy(
            src_ref=src.at[at],
            dst_ref=held.at[at],
            send_sem=rs_send.at[d * n + t],
            recv_sem=rs_recv.at[d * n + t],
            device_id={"ctx": ahead[d]},
            device_id_type=MESH,
        )

    def ag_copy(d, t):
        at = chunk_rows(d, t)
        return pltpu.make_async_remote_copy(
            src_ref=hid.at[at],
            dst_ref=hid.at[at],
            send_sem=ag_send.at[d * n + t],
            recv_sem=ag_recv.at[d * n + t],
            device_id={"ctx": ahead[1 - d]},
            device_id_type=MESH,
        )

    def gate_up(d, block):
        at = pl.ds(pl.multiple_of(d * half + block * BLOCK, BLOCK), BLOCK)

        @pl.loop(0, ff // tile)
        def _(c):
            base = pl.multiple_of(c * tile, tile)
            above = pl.multiple_of(ff + c * tile, tile)
            part[at, pl.ds(base, tile)] = jnp.dot(
                x[at, :], wg[:, pl.ds(base, tile)], preferred_element_type=jnp.float32
            ).astype(part.dtype)
            part[at, pl.ds(above, tile)] = jnp.dot(
                x[at, :], wu[:, pl.ds(base, tile)], preferred_element_type=jnp.float32
            ).astype(part.dtype)

    width = out.shape[1]
    down_tile = 256 if width % 256 == 0 else 128

    def down(d, block):
        at = pl.ds(pl.multiple_of(d * half + block * BLOCK, BLOCK), BLOCK)

        @pl.loop(0, width // down_tile)
        def _(c):
            cols = pl.ds(pl.multiple_of(c * down_tile, down_tile), down_tile)
            out[at, cols] = jnp.dot(
                hid[at, :], wd[:, cols], preferred_element_type=jnp.float32
            ).astype(out.dtype)

    first = (2 * p > last).astype(jnp.int32)
    loads[0].wait()
    loads[1].wait()
    gate_up(first, 0)

    @pl.loop(0, n + 2 * last)
    def _(s):
        for d in range(2):
            k = p if d == 0 else last - p
            t = s - k

            @pl.when((t >= 0) & (t < n))
            def _():
                at = chunk_rows(d, t)

                @pl.when(k == 0)
                def _():
                    rs_copy(d, t, part).start()

                @pl.when((k > 0) & (k < last))
                def _():
                    rs_copy(d, t, held).wait_recv()
                    held[at, :] = (
                        held[at, :].astype(jnp.float32) + part[at, :].astype(jnp.float32)
                    ).astype(held.dtype)
                    rs_copy(d, t, held).start()

                @pl.when(k == last)
                def _():
                    rs_copy(d, t, held).wait_recv()
                    gate = held[at, pl.ds(0, ff)].astype(jnp.float32) + part[
                        at, pl.ds(0, ff)
                    ].astype(jnp.float32)
                    up = held[at, pl.ds(ff, ff)].astype(jnp.float32) + part[
                        at, pl.ds(ff, ff)
                    ].astype(jnp.float32)
                    hid[at, :] = (gate / (1.0 + jnp.exp(-gate)) * up).astype(hid.dtype)
                    ag_copy(d, t).start()

        for d in range(2):
            j = last - p if d == 0 else p
            u = s - last - j

            @pl.when((u >= 0) & (u < n))
            def _():
                @pl.when(j > 0)
                def _():
                    ag_copy(d, u).wait_recv()

                    @pl.when(j < last)
                    def _():
                        ag_copy(d, u).start()

        i = s + 1

        @pl.when(i < 2 * blocks)
        def _():
            gate_up((i + first) % 2, i // 2)

        @pl.when(s == last)
        def _():
            loads[2].wait()

        for d in range(2):
            j = last - p if d == 0 else p
            u = s - last - j

            @pl.when((u >= 0) & (u < n) & (u % per == per - 1))
            def _():
                down(d, u // per)

    @pl.loop(0, n)
    def _(t):
        for d in range(2):
            k = p if d == 0 else last - p

            @pl.when(k < last)
            def _():
                rs_copy(d, t, held).wait_send()

            @pl.when(k > 0)
            def _():
                ag_copy(d, t).wait_send()


def expert_layer(rows_in, gate_w, up_w, down_w):
    n_ctx = lax.axis_size("ctx")
    rows, width = rows_in.shape
    ff = gate_w.shape[1]
    n = rows // 2 // CHUNK
    return pl.pallas_call(
        partial(expert_kernel, n_ctx),
        out_shape=jax.ShapeDtypeStruct((rows, width), jnp.bfloat16),
        in_specs=[pl.BlockSpec(memory_space=pltpu.VMEM)]
        + [pl.BlockSpec(memory_space=pl.ANY)] * 3,
        out_specs=pl.BlockSpec(memory_space=pltpu.VMEM),
        scratch_shapes=[
            pltpu.VMEM((width, ff), jnp.bfloat16),
            pltpu.VMEM((width, ff), jnp.bfloat16),
            pltpu.VMEM((ff, width), jnp.bfloat16),
            pltpu.VMEM((rows, 2 * ff), jnp.bfloat16),
            pltpu.VMEM((rows, 2 * ff), jnp.bfloat16),
            pltpu.VMEM((rows, ff), jnp.bfloat16),
            pltpu.SemaphoreType.DMA((3,)),
            pltpu.SemaphoreType.DMA((2 * n,)),
            pltpu.SemaphoreType.DMA((2 * n,)),
            pltpu.SemaphoreType.DMA((2 * n,)),
            pltpu.SemaphoreType.DMA((2 * n,)),
        ],
        compiler_params=pltpu.CompilerParams(
            collective_id=0, has_side_effects=True, vmem_limit_bytes=56 * 1024 * 1024
        ),
        cost_estimate=pl.CostEstimate(
            flops=6 * rows * width * ff, bytes_accessed=6 * width * ff, transcendentals=rows * ff
        ),
        name="expert_layer",
    )(rows_in, gate_w, up_w, down_w)


def score_block(running, pieces, key_start, query_latent, query_rope, query_pos, score_scale):
    running_max, running_sum, running_acc = running
    latent_piece, rope_piece = pieces
    scores = jnp.einsum(
        "ihc,jc->ihj", query_latent, latent_piece, preferred_element_type=jnp.float32
    )
    scores = scores + jnp.einsum(
        "ihr,jr->ihj", query_rope, rope_piece, preferred_element_type=jnp.float32
    )
    scores = scores * score_scale
    key_pos = jnp.arange(latent_piece.shape[0], dtype=jnp.int32)
    allowed = (key_pos[None, :] <= query_pos[:, None])[:, None, :]
    block_max = jnp.max(jnp.where(allowed, scores, NEG_FILL), axis=2)
    new_max = jnp.maximum(running_max, block_max)
    exp_terms = jnp.where(allowed, jnp.exp(scores - new_max[:, :, None]), 0.0)
    new_sum = jnp.sum(exp_terms, axis=2)
    update = jnp.einsum(
        "ihj,jc->ihc",
        exp_terms.astype(jnp.bfloat16),
        latent_piece,
        preferred_element_type=jnp.float32,
    )
    return (new_max, new_sum, update)


def local(
    q_nope,
    q_rope,
    kv_latent,
    key_rope,
    w_uk,
    w_uv,
    w_out,
    w_gate,
    w_up,
    w_down,
    route_ids,
    route_gates,
):
    tok_rows = q_nope.shape[0]
    head_count, nope_size, latent_size = w_uk.shape
    rope_size = key_rope.shape[1]
    score_scale = 1.0 / math.sqrt(nope_size + rope_size)
    ctx_here = lax.axis_index("ctx")
    query_pos = ctx_here * tok_rows + jnp.arange(tok_rows, dtype=jnp.int32)
    query_latent = jnp.einsum(
        "ihd,hdc->ihc",
        q_nope.reshape(tok_rows, head_count, nope_size),
        w_uk,
        preferred_element_type=jnp.float32,
    ).astype(jnp.bfloat16)
    query_rope = q_rope.reshape(tok_rows, head_count, rope_size)
    initial = (
        jnp.full((tok_rows, head_count), NEG_FILL, jnp.float32),
        jnp.zeros((tok_rows, head_count), jnp.float32),
        jnp.zeros((tok_rows, head_count, latent_size), jnp.float32),
    )
    step_fn = partial(
        score_block,
        query_latent=query_latent,
        query_rope=query_rope,
        query_pos=query_pos,
        score_scale=score_scale,
    )
    attended = step_fn(
        initial,
        (
            lax.all_gather(kv_latent, "ctx", axis=0, tiled=True),
            lax.all_gather(key_rope, "ctx", axis=0, tiled=True),
        ),
        jnp.int32(0),
    )
    latent_out = (attended[2] / attended[1][:, :, None]).astype(jnp.bfloat16)
    head_out = jnp.einsum(
        "ihc,hcv->ihv", latent_out, w_uv, preferred_element_type=jnp.float32
    ).astype(jnp.bfloat16)
    gathered = lax.all_gather(head_out.reshape(tok_rows, -1), "ctx", axis=0, tiled=True)
    out_rows = gathered.shape[0] // lax.axis_size("exp")
    attn_out = lax.psum_scatter(
        jnp.dot(gathered, w_out, preferred_element_type=jnp.float32).astype(jnp.bfloat16),
        "exp",
        scatter_dimension=0,
        tiled=True,
    )
    feature_cols = attn_out.shape[1]
    top_count = route_ids.shape[1]
    expert_count = lax.axis_size("exp") * w_gate.shape[0]
    capacity = 3 * out_rows * top_count // (2 * expert_count)
    slot_total = expert_count * capacity
    flat_ids = route_ids.reshape(-1)
    onehot = (flat_ids[:, None] == jnp.arange(expert_count, dtype=jnp.int32)[None, :]).astype(
        jnp.int32
    )
    earlier = jnp.cumsum(onehot, axis=0) - onehot
    slot_ids = jnp.sum(earlier * onehot, axis=1)
    targets = (flat_ids * capacity + slot_ids).reshape(out_rows, top_count)
    slot_range = jnp.arange(slot_total, dtype=jnp.int32)
    hits = targets[:, :, None] == slot_range[None, None, :]
    placing = jnp.sum(hits.astype(jnp.float32), axis=1).astype(jnp.bfloat16).T
    send_rows = jnp.dot(placing, attn_out, preferred_element_type=jnp.float32).astype(jnp.bfloat16)
    send_rows = send_rows.reshape(expert_count, capacity, feature_cols)
    weighting = jnp.sum(
        jnp.where(hits, route_gates[:, :, None], jnp.zeros((), jnp.bfloat16)), axis=1
    )
    arrived = lax.all_to_all(send_rows, "exp", split_axis=0, concat_axis=0, tiled=True)
    source_count = arrived.shape[0]
    item_count = arrived.shape[1]
    flat_rows = arrived.reshape(source_count * item_count, feature_cols)
    expert_out = expert_layer(flat_rows, w_gate[0], w_up[0], w_down[0])
    expert_out = expert_out.reshape(source_count, item_count, feature_cols)
    returned = lax.all_to_all(expert_out, "exp", split_axis=0, concat_axis=0, tiled=True)
    moe_out = jnp.dot(
        weighting, returned.reshape(slot_total, feature_cols), preferred_element_type=jnp.float32
    ).astype(jnp.bfloat16)
    return (attn_out, moe_out)


def solution(mesh):
    placed = (
        P("ctx", "exp"),
        P("ctx", "exp"),
        P("ctx", None),
        P("ctx", None),
        P("exp", None, None),
        P("exp", None, None),
        P("exp", "ctx"),
        P("exp", "ctx", None),
        P("exp", "ctx", None),
        P("exp", None, "ctx"),
        P("exp", None),
        P("exp", None),
    )
    return jax.shard_map(
        local,
        mesh=mesh,
        in_specs=placed,
        out_specs=(P("exp", "ctx"), P("exp", "ctx")),
        check_vma=False,
    )
```

```python
from functools import partial
import math

import jax
import jax.numpy as jnp
from jax import lax
from jax.experimental import pallas as pl
from jax.experimental.pallas import tpu as pltpu
from jax.sharding import PartitionSpec as P

NEG_FILL = -1e30
MESH = pl.DeviceIdType.MESH
CHUNK = 16
BLOCK = 128


def expert_kernel(
    n_ctx, x, wg_hbm, wu_hbm, wd_hbm, out, wg, wu, wd, part, held, hid,
    w_sem, rs_send, rs_recv, ag_send, ag_recv,
):
    p = lax.axis_index("ctx")
    last = n_ctx - 1
    rows = x.shape[0]
    half = rows // 2
    ff = wg.shape[1]
    n = half // CHUNK
    per = BLOCK // CHUNK
    blocks = half // BLOCK
    tile = 512 if ff % 512 == 0 else ff

    loads = [
        pltpu.make_async_copy(src, dst, w_sem.at[i])
        for i, (src, dst) in enumerate(((wg_hbm, wg), (wu_hbm, wu), (wd_hbm, wd)))
    ]
    for load in loads:
        load.start()

    barrier = pltpu.get_barrier_semaphore()

    @pl.when(p > 0)
    def _():
        pl.semaphore_signal(barrier, inc=1, device_id={"ctx": p - 1}, device_id_type=MESH)

    @pl.when(p < last)
    def _():
        pl.semaphore_signal(barrier, inc=1, device_id={"ctx": p + 1}, device_id_type=MESH)

    pl.semaphore_wait(barrier, (p > 0).astype(jnp.int32) + (p < last).astype(jnp.int32))

    ahead = (jnp.minimum(p + 1, last), jnp.maximum(p - 1, 0))

    def chunk_rows(d, t):
        return pl.ds(pl.multiple_of(d * half + t * CHUNK, CHUNK), CHUNK)

    def rs_copy(d, t, src):
        at = chunk_rows(d, t)
        return pltpu.make_async_remote_copy(
            src_ref=src.at[at],
            dst_ref=held.at[at],
            send_sem=rs_send.at[d * n + t],
            recv_sem=rs_recv.at[d * n + t],
            device_id={"ctx": ahead[d]},
            device_id_type=MESH,
        )

    def ag_copy(d, t):
        at = chunk_rows(d, t)
        return pltpu.make_async_remote_copy(
            src_ref=hid.at[at],
            dst_ref=hid.at[at],
            send_sem=ag_send.at[d * n + t],
            recv_sem=ag_recv.at[d * n + t],
            device_id={"ctx": ahead[1 - d]},
            device_id_type=MESH,
        )

    def gate_up(d, block):
        at = pl.ds(pl.multiple_of(d * half + block * BLOCK, BLOCK), BLOCK)

        @pl.loop(0, ff // tile)
        def _(c):
            base = pl.multiple_of(c * tile, tile)
            above = pl.multiple_of(ff + c * tile, tile)
            part[at, pl.ds(base, tile)] = jnp.dot(
                x[at, :], wg[:, pl.ds(base, tile)], preferred_element_type=jnp.float32
            ).astype(part.dtype)
            part[at, pl.ds(above, tile)] = jnp.dot(
                x[at, :], wu[:, pl.ds(base, tile)], preferred_element_type=jnp.float32
            ).astype(part.dtype)

    width = out.shape[1]
    down_tile = 256 if width % 256 == 0 else 128

    def down(d, block):
        at = pl.ds(pl.multiple_of(d * half + block * BLOCK, BLOCK), BLOCK)

        @pl.loop(0, width // down_tile)
        def _(c):
            cols = pl.ds(pl.multiple_of(c * down_tile, down_tile), down_tile)
            out[at, cols] = jnp.dot(
                hid[at, :], wd[:, cols], preferred_element_type=jnp.float32
            ).astype(out.dtype)

    first = (2 * p > last).astype(jnp.int32)
    loads[0].wait()
    loads[1].wait()
    gate_up(first, 0)

    @pl.loop(0, n + 2 * last)
    def _(s):
        for d in range(2):
            k = p if d == 0 else last - p
            t = s - k

            @pl.when((t >= 0) & (t < n))
            def _():
                at = chunk_rows(d, t)

                @pl.when(k == 0)
                def _():
                    rs_copy(d, t, part).start()

                @pl.when((k > 0) & (k < last))
                def _():
                    rs_copy(d, t, held).wait_recv()
                    held[at, :] = (
                        held[at, :].astype(jnp.float32) + part[at, :].astype(jnp.float32)
                    ).astype(held.dtype)
                    rs_copy(d, t, held).start()

                @pl.when(k == last)
                def _():
                    rs_copy(d, t, held).wait_recv()
                    gate = held[at, pl.ds(0, ff)].astype(jnp.float32) + part[
                        at, pl.ds(0, ff)
                    ].astype(jnp.float32)
                    up = held[at, pl.ds(ff, ff)].astype(jnp.float32) + part[
                        at, pl.ds(ff, ff)
                    ].astype(jnp.float32)
                    hid[at, :] = (gate / (1.0 + jnp.exp(-gate)) * up).astype(hid.dtype)
                    ag_copy(d, t).start()

        for d in range(2):
            j = last - p if d == 0 else p
            u = s - last - j

            @pl.when((u >= 0) & (u < n))
            def _():
                @pl.when(j > 0)
                def _():
                    ag_copy(d, u).wait_recv()

                    @pl.when(j < last)
                    def _():
                        ag_copy(d, u).start()

        i = s + 1

        @pl.when(i < 2 * blocks)
        def _():
            gate_up((i + first) % 2, i // 2)

        @pl.when(s == last)
        def _():
            loads[2].wait()

        for d in range(2):
            j = last - p if d == 0 else p
            u = s - last - j

            @pl.when((u >= 0) & (u < n) & (u % per == per - 1))
            def _():
                down(d, u // per)

    @pl.loop(0, n)
    def _(t):
        for d in range(2):
            k = p if d == 0 else last - p

            @pl.when(k < last)
            def _():
                rs_copy(d, t, held).wait_send()

            @pl.when(k > 0)
            def _():
                ag_copy(d, t).wait_send()


def expert_layer(rows_in, gate_w, up_w, down_w):
    n_ctx = lax.axis_size("ctx")
    rows, width = rows_in.shape
    ff = gate_w.shape[1]
    n = rows // 2 // CHUNK
    return pl.pallas_call(
        partial(expert_kernel, n_ctx),
        out_shape=jax.ShapeDtypeStruct((rows, width), jnp.bfloat16),
        in_specs=[pl.BlockSpec(memory_space=pltpu.VMEM)]
        + [pl.BlockSpec(memory_space=pl.ANY)] * 3,
        out_specs=pl.BlockSpec(memory_space=pltpu.VMEM),
        scratch_shapes=[
            pltpu.VMEM((width, ff), jnp.bfloat16),
            pltpu.VMEM((width, ff), jnp.bfloat16),
            pltpu.VMEM((ff, width), jnp.bfloat16),
            pltpu.VMEM((rows, 2 * ff), jnp.bfloat16),
            pltpu.VMEM((rows, 2 * ff), jnp.bfloat16),
            pltpu.VMEM((rows, ff), jnp.bfloat16),
            pltpu.SemaphoreType.DMA((3,)),
            pltpu.SemaphoreType.DMA((2 * n,)),
            pltpu.SemaphoreType.DMA((2 * n,)),
            pltpu.SemaphoreType.DMA((2 * n,)),
            pltpu.SemaphoreType.DMA((2 * n,)),
        ],
        compiler_params=pltpu.CompilerParams(
            collective_id=0, has_side_effects=True, vmem_limit_bytes=56 * 1024 * 1024
        ),
        cost_estimate=pl.CostEstimate(
            flops=6 * rows * width * ff, bytes_accessed=6 * width * ff, transcendentals=rows * ff
        ),
        name="expert_layer",
    )(rows_in, gate_w, up_w, down_w)

def attend_kernel(
    n_ctx, score_scale, q_nope, q_rope, kv, w_uk, w_uv, wo_hbm, out, keys, queries, heads, acc, wo,
    w_sem, kv_send, kv_recv, core_send, core_recv, h_send, h_recv,
):
    p = lax.axis_index("ctx")
    e = lax.axis_index("exp")
    last = n_ctx - 1
    half = e % 2
    sibling = e + 1 - 2 * half
    tok = q_nope.shape[0]
    part = tok // 2
    head_count, nope, lat = w_uk.shape
    vhead = w_uv.shape[2]
    rope2 = kv.shape[1] - lat
    pairs = head_count // 2
    total = keys.shape[0]

    load = pltpu.make_async_copy(wo_hbm, wo, w_sem)
    load.start()

    barrier = pltpu.get_barrier_semaphore()
    for o in range(n_ctx):

        @pl.when(p != o)
        def _():
            pl.semaphore_signal(barrier, inc=1, device_id={"ctx": o}, device_id_type=MESH)

    pl.semaphore_signal(barrier, inc=1, device_id={"exp": sibling}, device_id_type=MESH)
    pl.semaphore_wait(barrier, n_ctx)

    def kv_copy(i):
        return pltpu.make_async_remote_copy(
            src_ref=kv.at[pl.ds(pl.multiple_of(half * part, part), part)],
            dst_ref=keys.at[pl.ds(pl.multiple_of(p * tok + half * part, part), part)],
            send_sem=kv_send.at[i],
            recv_sem=kv_recv.at[p],
            device_id={"ctx": jnp.minimum(p + 1 + i, last)},
            device_id_type=MESH,
        )

    def kv_arrival(o):
        at = pl.ds(pl.multiple_of(o * tok + half * part, part), part)
        return pltpu.make_async_remote_copy(
            src_ref=keys.at[at],
            dst_ref=keys.at[at],
            send_sem=kv_send.at[0],
            recv_sem=kv_recv.at[o],
            device_id={"ctx": jnp.maximum(p - 1, 0)},
            device_id_type=MESH,
        )

    def core_copy(o, side):
        at = pl.ds(pl.multiple_of(o * tok + side * part, part), part)
        return pltpu.make_async_remote_copy(
            src_ref=keys.at[at],
            dst_ref=keys.at[at],
            send_sem=core_send.at[o],
            recv_sem=core_recv.at[o],
            device_id={"exp": sibling},
            device_id_type=MESH,
        )

    for i in range(last):

        @pl.when(p + 1 + i <= last)
        def _():
            kv_copy(i).start()

    for o in range(n_ctx):

        @pl.when(p == o)
        def _():
            keys[pl.ds(o * tok, tok), :] = kv[...]

        @pl.when(p < o)
        def _():
            keys[pl.ds(o * tok, tok), :] = jnp.zeros((tok, keys.shape[1]), keys.dtype)

    @pl.loop(0, pairs)
    def _(s):
        rope = q_rope[:, pl.ds(pl.multiple_of(s * rope2, rope2), rope2)]
        lane = lax.broadcasted_iota(jnp.int32, rope.shape, 1)
        for a in range(2):
            h = 2 * s + a
            queries[h, :, pl.ds(0, lat)] = jnp.dot(
                q_nope[:, pl.ds(pl.multiple_of(h * nope, nope), nope)],
                w_uk[h],
                preferred_element_type=jnp.float32,
            ).astype(queries.dtype)
            own = (lane < rope2 // 2) if a == 0 else (lane >= rope2 // 2)
            queries[h, :, pl.ds(lat, rope2)] = jnp.where(own, rope, jnp.zeros_like(rope))

    for o in reversed(range(last)):

        @pl.when(o < p)
        def _():
            kv_arrival(o).wait_recv()
            core_copy(o, half).start()

    for o in reversed(range(last)):

        @pl.when(o < p)
        def _():
            core_copy(o, 1 - half).wait_recv()

    def head_copy(way, o, t):
        at = pl.ds(pl.multiple_of(o * tok, tok), tok)
        cols = pl.ds(pl.multiple_of((t % 2) * 2 * vhead, 2 * vhead), 2 * vhead)
        there = jnp.minimum(p + 1, last) if way == 0 else jnp.maximum(p - 1, 0)
        return pltpu.make_async_remote_copy(
            src_ref=heads.at[t // 2, at, cols],
            dst_ref=heads.at[t // 2, at, cols],
            send_sem=h_send.at[(way * n_ctx + o) * pairs + t],
            recv_sem=h_recv.at[o * pairs + t],
            device_id={"ctx": there},
            device_id_type=MESH,
        )

    query_pos = p * tok + lax.broadcasted_iota(jnp.int32, (tok, total), 0)
    key_pos = lax.broadcasted_iota(jnp.int32, (tok, total), 1)

    @pl.loop(0, pairs + n_ctx - 2)
    def _(s):
        @pl.when(s < pairs)
        def _():
            for a in range(2):
                h = 2 * s + a
                scores = lax.dot_general(
                    queries[h],
                    keys[...],
                    (((1,), (1,)), ((), ())),
                    preferred_element_type=jnp.float32,
                )
                scores = jnp.where(key_pos <= query_pos, scores * score_scale, NEG_FILL)
                terms = jnp.exp(scores - jnp.max(scores, axis=1, keepdims=True))
                sums = jnp.sum(terms, axis=1, keepdims=True)
                mixed = jnp.dot(
                    terms.astype(jnp.bfloat16),
                    keys[:, pl.ds(0, lat)],
                    preferred_element_type=jnp.float32,
                )
                latent_out = (mixed / sums).astype(jnp.bfloat16)
                cols = pl.ds(
                    pl.multiple_of((s % 2) * 2 * vhead + a * vhead, vhead), vhead
                )
                heads[s // 2, pl.ds(pl.multiple_of(p * tok, tok), tok), cols] = jnp.dot(
                    latent_out, w_uv[h], preferred_element_type=jnp.float32
                ).astype(heads.dtype)

            @pl.when(p < last)
            def _():
                head_copy(0, p, s).start()

            @pl.when(p > 0)
            def _():
                head_copy(1, p, s).start()

        for k in range(1, n_ctx - 1):
            t = s - k

            @pl.when((t >= 0) & (t < pairs) & (p - k >= 0) & (p < last))
            def _():
                head_copy(0, p - k, t).wait_recv()
                head_copy(0, p - k, t).start()

            @pl.when((t >= 0) & (t < pairs) & (p + k <= last) & (p > 0))
            def _():
                head_copy(1, p + k, t).wait_recv()
                head_copy(1, p + k, t).start()

    load.wait()
    width = out.shape[1]
    tile = 256 if width % 256 == 0 else 128
    depth = 4 * vhead
    groups = pairs // 2
    for g in range(groups):
        for t in (2 * g, 2 * g + 1):

            @pl.when(p == last)
            def _():
                for o in range(last):
                    head_copy(0, o, t).wait_recv()

            @pl.when(p == 0)
            def _():
                for o in range(1, n_ctx):
                    head_copy(1, o, t).wait_recv()

        @pl.loop(0, width // tile)
        def _(c):
            cols = pl.ds(pl.multiple_of(c * tile, tile), tile)
            term = jnp.dot(
                heads[g], wo[pl.ds(g * depth, depth), cols], preferred_element_type=jnp.float32
            )
            if g > 0:
                term = acc[:, cols] + term
            if g < groups - 1:
                acc[:, cols] = term
            else:
                out[:, cols] = term.astype(out.dtype)

    for i in range(last):

        @pl.when(p + 1 + i <= last)
        def _():
            kv_copy(i).wait_send()

        @pl.when(i < p)
        def _():
            core_copy(i, half).wait_send()

    @pl.loop(0, pairs)
    def _(t):
        for o in range(n_ctx):

            @pl.when((o <= p) & (p < last))
            def _():
                head_copy(0, o, t).wait_send()

            @pl.when((o >= p) & (p > 0))
            def _():
                head_copy(1, o, t).wait_send()


def attend(q_nope, q_rope, kv, w_uk, w_uv, w_out, score_scale):
    n_ctx = lax.axis_size("ctx")
    tok = q_nope.shape[0]
    head_count, nope, lat = w_uk.shape
    vhead = w_uv.shape[2]
    pairs = head_count // 2
    total = n_ctx * tok
    width = w_out.shape[1]
    dma = pltpu.SemaphoreType.DMA
    return pl.pallas_call(
        partial(attend_kernel, n_ctx, score_scale),
        out_shape=jax.ShapeDtypeStruct((total, width), jnp.bfloat16),
        in_specs=[pl.BlockSpec(memory_space=pltpu.VMEM)] * 5
        + [pl.BlockSpec(memory_space=pl.ANY)],
        out_specs=pl.BlockSpec(memory_space=pltpu.VMEM),
        scratch_shapes=[
            pltpu.VMEM((total, kv.shape[1]), jnp.bfloat16),
            pltpu.VMEM((head_count, tok, kv.shape[1]), jnp.bfloat16),
            pltpu.VMEM((pairs // 2, total, 4 * vhead), jnp.bfloat16),
            pltpu.VMEM((total, width), jnp.float32),
            pltpu.VMEM(w_out.shape, jnp.bfloat16),
            dma,
            dma((n_ctx,)),
            dma((n_ctx,)),
            dma((n_ctx,)),
            dma((n_ctx,)),
            dma((2 * n_ctx * pairs,)),
            dma((n_ctx * pairs,)),
        ],
        compiler_params=pltpu.CompilerParams(
            collective_id=1, has_side_effects=True, vmem_limit_bytes=56 * 1024 * 1024
        ),
        cost_estimate=pl.CostEstimate(
            flops=2 * total * width * w_out.shape[0],
            bytes_accessed=2 * w_out.size,
            transcendentals=head_count * tok * total,
        ),
        name="attend",
    )(q_nope, q_rope, kv, w_uk, w_uv, w_out)


def exp_kernel(bits, cols, spread, *refs):
    refs = list(refs)
    mine = refs.pop(0)
    extra = refs.pop(0) if spread else None
    out = refs.pop(0)
    every = refs.pop(0) if spread else None
    sums = [[refs.pop(0) for _ in range(bits)] for _ in cols]
    came = [[refs.pop(0) for _ in range(bits)] for _ in cols]
    rs_send, rs_recv = refs.pop(0), refs.pop(0)
    if spread:
        ag_send, ag_recv = refs.pop(0), refs.pop(0)

    e = lax.axis_index("exp")
    bit = [(e // (1 << b)) % 2 for b in range(bits)]
    partner = [e + (1 - 2 * bit[b]) * (1 << b) for b in range(bits)]
    orders = [list(range(bits)), [0] + list(range(bits - 1, 0, -1))]

    barrier = pltpu.get_barrier_semaphore()
    for b in range(bits):
        pl.semaphore_signal(barrier, inc=1, device_id={"exp": partner[b]}, device_id_type=MESH)
    pl.semaphore_wait(barrier, bits)

    def place(free, at):
        return tuple(at.get(b, slice(None)) for b in free)

    copies = []
    for j in range(bits):
        stage = []
        for f, (start, size) in enumerate(cols):
            b = orders[f][j]
            free = [x for x in range(bits - 1, -1, -1) if x not in orders[f][:j]]
            there = place(free, {b: 1 - bit[b]})
            if j == 0:
                src = mine.at[there + (slice(None), pl.ds(start, size))]
            else:
                src = sums[f][j - 1].at[there]
            copy = pltpu.make_async_remote_copy(
                src_ref=src,
                dst_ref=came[f][j],
                send_sem=rs_send.at[f * bits + j],
                recv_sem=rs_recv.at[f * bits + j],
                device_id={"exp": partner[b]},
                device_id_type=MESH,
            )
            copy.start()
            stage.append(copy)
        for f, (start, size) in enumerate(cols):
            b = orders[f][j]
            free = [x for x in range(bits - 1, -1, -1) if x not in orders[f][:j]]
            here = place(free, {b: bit[b]})
            stage[f].wait_recv()
            if j == 0:
                own = mine[here + (slice(None), pl.ds(start, size))]
            else:
                own = sums[f][j - 1][here]
            sums[f][j][...] = (
                own.astype(jnp.float32) + came[f][j][...].astype(jnp.float32)
            ).astype(jnp.bfloat16)
        copies += stage

    spot = tuple(bit[b] for b in range(bits - 1, -1, -1))
    for f, (start, size) in enumerate(cols):
        out[:, pl.ds(start, size)] = sums[f][bits - 1][...]
        if spread:
            every[spot + (slice(None), pl.ds(start, size))] = sums[f][bits - 1][...]
    if spread:
        width = mine.shape[-1]
        more = extra.shape[-1]
        every[spot + (slice(None), pl.ds(width, more))] = extra[...]
        for j in reversed(range(bits)):
            stage = []
            for f, (start, size) in enumerate(cols):
                size = size + (more if f == 1 else 0)
                at = place(range(bits - 1, -1, -1), {b: bit[b] for b in orders[f][: j + 1]})
                block = every.at[at + (slice(None), pl.ds(start, size))]
                copy = pltpu.make_async_remote_copy(
                    src_ref=block,
                    dst_ref=block,
                    send_sem=ag_send.at[f * bits + j],
                    recv_sem=ag_recv.at[f * bits + j],
                    device_id={"exp": partner[orders[f][j]]},
                    device_id_type=MESH,
                )
                copy.start()
                stage.append(copy)
            for copy in stage:
                copy.wait_recv()
            copies += stage
    for copy in copies:
        copy.wait_send()


def exp_sum(rows_in, extra, collective_id):
    n_exp = lax.axis_size("exp")
    bits = n_exp.bit_length() - 1
    total, width = rows_in.shape
    rows = total // n_exp
    spread = extra is not None
    first = (width // 2 + 127) // 128 * 128
    cols = ((0, first), (first, width - first))
    vmem = pl.BlockSpec(memory_space=pltpu.VMEM)
    shapes = []
    for _ in range(2):
        for _, size in cols:
            for j in range(bits):
                shapes.append(pltpu.VMEM((2,) * (bits - 1 - j) + (rows, size), jnp.bfloat16))
    shapes += [pltpu.SemaphoreType.DMA((2 * bits,))] * (4 if spread else 2)
    out_shape = [jax.ShapeDtypeStruct((rows, width), jnp.bfloat16)]
    operands = [rows_in.reshape((2,) * bits + (rows, width))]
    if spread:
        wide = width + extra.shape[1]
        out_shape.append(jax.ShapeDtypeStruct((2,) * bits + (rows, wide), jnp.bfloat16))
        operands.append(extra)
    got = pl.pallas_call(
        partial(exp_kernel, bits, cols, spread),
        out_shape=out_shape,
        in_specs=[vmem] * len(operands),
        out_specs=[vmem] * len(out_shape),
        scratch_shapes=shapes,
        compiler_params=pltpu.CompilerParams(
            collective_id=collective_id, has_side_effects=True, vmem_limit_bytes=40 * 1024 * 1024
        ),
        cost_estimate=pl.CostEstimate(
            flops=2 * total * width, bytes_accessed=4 * total * width, transcendentals=0
        ),
        name="exp_sum_spread" if spread else "exp_sum",
    )(*operands)
    if spread:
        return got[0], got[1].reshape(total, wide)
    return got[0]


def local(
    q_nope,
    q_rope,
    kv_latent,
    key_rope,
    w_uk,
    w_uv,
    w_out,
    w_gate,
    w_up,
    w_down,
    route_ids,
    route_gates,
):
    nope_size = w_uk.shape[1]
    rope_size = key_rope.shape[1]
    n_exp = lax.axis_size("exp")
    keys = jnp.concatenate([kv_latent, key_rope, key_rope], axis=1)
    partial_out = attend(
        q_nope, q_rope, keys, w_uk, w_uv, w_out, 1.0 / math.sqrt(nope_size + rope_size)
    )
    out_rows, top_count = route_ids.shape
    routing = jnp.concatenate([route_ids.astype(jnp.bfloat16), route_gates], axis=1)
    routing = jnp.pad(routing, ((0, 0), (0, 128 - 2 * top_count)))
    attn_out, gathered = exp_sum(partial_out, routing, 2)
    total, width = partial_out.shape
    capacity = 3 * out_rows * top_count // (2 * n_exp)
    slot_total = n_exp * capacity
    ids = gathered[:, width : width + top_count].astype(jnp.float32)
    gates = gathered[:, width + top_count : width + 2 * top_count].astype(jnp.float32)
    named = ids == lax.axis_index("exp").astype(jnp.float32)
    chosen = jnp.any(named, axis=1)
    gate = jnp.sum(jnp.where(named, gates, 0.0), axis=1)
    below = jnp.tril(jnp.ones((out_rows, out_rows), jnp.bfloat16), -1)
    ranks = lax.dot_general(
        chosen.astype(jnp.bfloat16).reshape(n_exp, out_rows),
        below,
        (((1,), (1,)), ((), ())),
        preferred_element_type=jnp.float32,
    ).astype(jnp.int32)
    slots = ranks + capacity * jnp.arange(n_exp, dtype=jnp.int32)[:, None]
    slots = jnp.where(chosen, slots.reshape(total), -1)
    slot_range = jnp.arange(slot_total, dtype=jnp.int32)
    placing = (slots[None, :] == slot_range[:, None]).astype(jnp.bfloat16)
    arrived = jnp.dot(
        placing, gathered[:, :width], preferred_element_type=jnp.float32
    ).astype(jnp.bfloat16)
    expert_out = expert_layer(arrived, w_gate[0], w_up[0], w_down[0])
    weighting = jnp.where(slots[:, None] == slot_range[None, :], gate[:, None], 0.0)
    share = jnp.dot(
        weighting.astype(jnp.bfloat16), expert_out, preferred_element_type=jnp.float32
    ).astype(jnp.bfloat16)
    return (attn_out, exp_sum(share, None, 3))


def solution(mesh):
    placed = (
        P("ctx", "exp"),
        P("ctx", "exp"),
        P("ctx", None),
        P("ctx", None),
        P("exp", None, None),
        P("exp", None, None),
        P("exp", "ctx"),
        P("exp", "ctx", None),
        P("exp", "ctx", None),
        P("exp", None, "ctx"),
        P("exp", None),
        P("exp", None),
    )
    return jax.shard_map(
        local,
        mesh=mesh,
        in_specs=placed,
        out_specs=(P("exp", "ctx"), P("exp", "ctx")),
        check_vma=False,
    )
```

```python
from functools import partial
import math

import jax
import jax.numpy as jnp
from jax import lax
from jax.experimental import pallas as pl
from jax.experimental.pallas import tpu as pltpu
from jax.sharding import PartitionSpec as P

NEG_FILL = -1e30
MESH = pl.DeviceIdType.MESH
CHUNK = 16
SLACK = 2
AHEAD = 3
BLOCK = 128


def expert_kernel(
    n_ctx, x, wg_hbm, wu_hbm, wd_hbm, out, wg, wu, wd, part, held, hid,
    w_sem, rs_send, rs_recv, ag_send, ag_recv,
):
    p = lax.axis_index("ctx")
    last = n_ctx - 1
    rows = x.shape[0]
    half = rows // 2
    ff = wg.shape[1]
    n = half // CHUNK
    per = BLOCK // CHUNK
    blocks = half // BLOCK
    tile = 512 if ff % 512 == 0 else ff

    tiles = ff // tile
    loads = []
    for c in range(tiles):
        cols = pl.ds(c * tile, tile)
        for src, dst in ((wg_hbm, wg), (wu_hbm, wu)):
            loads.append(
                pltpu.make_async_copy(src.at[:, cols], dst.at[:, cols], w_sem.at[len(loads)])
            )
    loads.append(pltpu.make_async_copy(wd_hbm, wd, w_sem.at[len(loads)]))
    for load in loads:
        load.start()

    barrier = pltpu.get_barrier_semaphore()

    @pl.when(p > 0)
    def _():
        pl.semaphore_signal(barrier, inc=1, device_id={"ctx": p - 1}, device_id_type=MESH)

    @pl.when(p < last)
    def _():
        pl.semaphore_signal(barrier, inc=1, device_id={"ctx": p + 1}, device_id_type=MESH)

    pl.semaphore_wait(barrier, (p > 0).astype(jnp.int32) + (p < last).astype(jnp.int32))

    ahead = (jnp.minimum(p + 1, last), jnp.maximum(p - 1, 0))

    def chunk_rows(d, t):
        return pl.ds(pl.multiple_of(d * half + t * CHUNK, CHUNK), CHUNK)

    def rs_copy(d, t, src):
        at = chunk_rows(d, t)
        return pltpu.make_async_remote_copy(
            src_ref=src.at[at],
            dst_ref=held.at[at],
            send_sem=rs_send.at[d * n + t],
            recv_sem=rs_recv.at[d * n + t],
            device_id={"ctx": ahead[d]},
            device_id_type=MESH,
        )

    def ag_copy(d, t):
        at = chunk_rows(d, t)
        return pltpu.make_async_remote_copy(
            src_ref=hid.at[at],
            dst_ref=hid.at[at],
            send_sem=ag_send.at[d * n + t],
            recv_sem=ag_recv.at[d * n + t],
            device_id={"ctx": ahead[1 - d]},
            device_id_type=MESH,
        )

    def gate_up_tile(d, block, c):
        at = pl.ds(pl.multiple_of(d * half + block * BLOCK, BLOCK), BLOCK)
        base = pl.multiple_of(c * tile, tile)
        above = pl.multiple_of(ff + c * tile, tile)
        part[at, pl.ds(base, tile)] = jnp.dot(
            x[at, :], wg[:, pl.ds(base, tile)], preferred_element_type=jnp.float32
        ).astype(part.dtype)
        part[at, pl.ds(above, tile)] = jnp.dot(
            x[at, :], wu[:, pl.ds(base, tile)], preferred_element_type=jnp.float32
        ).astype(part.dtype)

    def gate_up(d, block):
        @pl.loop(0, tiles)
        def _(c):
            gate_up_tile(d, block, c)

    width = out.shape[1]
    down_tile = 256 if width % 256 == 0 else 128

    def down(d, block):
        at = pl.ds(pl.multiple_of(d * half + block * BLOCK, BLOCK), BLOCK)

        @pl.loop(0, width // down_tile)
        def _(c):
            cols = pl.ds(pl.multiple_of(c * down_tile, down_tile), down_tile)
            out[at, cols] = jnp.dot(
                hid[at, :], wd[:, cols], preferred_element_type=jnp.float32
            ).astype(out.dtype)

    first = (2 * p > last).astype(jnp.int32)
    for c in range(tiles):
        loads[2 * c].wait()
        loads[2 * c + 1].wait()
        gate_up_tile(first, 0, c)

    @pl.loop(0, n + 2 * last * SLACK)
    def _(s):
        for d in range(2):
            k = p if d == 0 else last - p
            t = s - k * SLACK

            @pl.when((t >= 0) & (t < n))
            def _():
                at = chunk_rows(d, t)

                @pl.when((k == 0) & (t >= AHEAD))
                def _():
                    rs_copy(d, t - AHEAD, part).wait_send()

                @pl.when(k == 0)
                def _():
                    rs_copy(d, t, part).start()

                @pl.when((k > 0) & (k < last))
                def _():
                    rs_copy(d, t, held).wait_recv()
                    held[at, :] = (
                        held[at, :].astype(jnp.float32) + part[at, :].astype(jnp.float32)
                    ).astype(held.dtype)
                    rs_copy(d, t, held).start()

                @pl.when(k == last)
                def _():
                    rs_copy(d, t, held).wait_recv()
                    gate = held[at, pl.ds(0, ff)].astype(jnp.float32) + part[
                        at, pl.ds(0, ff)
                    ].astype(jnp.float32)
                    up = held[at, pl.ds(ff, ff)].astype(jnp.float32) + part[
                        at, pl.ds(ff, ff)
                    ].astype(jnp.float32)
                    hid[at, :] = (gate / (1.0 + jnp.exp(-gate)) * up).astype(hid.dtype)
                    ag_copy(d, t).start()

        for d in range(2):
            j = last - p if d == 0 else p
            u = s - (last + j) * SLACK

            @pl.when((u >= 0) & (u < n))
            def _():
                @pl.when(j > 0)
                def _():
                    ag_copy(d, u).wait_recv()

                    @pl.when(j < last)
                    def _():
                        ag_copy(d, u).start()

        i = s + 1

        @pl.when(i < 2 * blocks)
        def _():
            gate_up((i + first) % 2, i // 2)

        @pl.when(s == last)
        def _():
            loads[-1].wait()

        for d in range(2):
            j = last - p if d == 0 else p
            u = s - (last + j) * SLACK

            @pl.when((u >= 0) & (u < n) & (u % per == per - 1))
            def _():
                down(d, u // per)

    @pl.loop(0, n)
    def _(t):
        for d in range(2):
            k = p if d == 0 else last - p

            @pl.when((k < last) & ((k > 0) | (t >= n - AHEAD)))
            def _():
                rs_copy(d, t, held).wait_send()

            @pl.when(k > 0)
            def _():
                ag_copy(d, t).wait_send()


def expert_layer(rows_in, gate_w, up_w, down_w):
    n_ctx = lax.axis_size("ctx")
    rows, width = rows_in.shape
    ff = gate_w.shape[1]
    n = rows // 2 // CHUNK
    return pl.pallas_call(
        partial(expert_kernel, n_ctx),
        out_shape=jax.ShapeDtypeStruct((rows, width), jnp.bfloat16),
        in_specs=[pl.BlockSpec(memory_space=pltpu.VMEM)]
        + [pl.BlockSpec(memory_space=pl.ANY)] * 3,
        out_specs=pl.BlockSpec(memory_space=pltpu.VMEM),
        scratch_shapes=[
            pltpu.VMEM((width, ff), jnp.bfloat16),
            pltpu.VMEM((width, ff), jnp.bfloat16),
            pltpu.VMEM((ff, width), jnp.bfloat16),
            pltpu.VMEM((rows, 2 * ff), jnp.bfloat16),
            pltpu.VMEM((rows, 2 * ff), jnp.bfloat16),
            pltpu.VMEM((rows, ff), jnp.bfloat16),
            pltpu.SemaphoreType.DMA((2 * max(1, ff // 512) + 1,)),
            pltpu.SemaphoreType.DMA((2 * n,)),
            pltpu.SemaphoreType.DMA((2 * n,)),
            pltpu.SemaphoreType.DMA((2 * n,)),
            pltpu.SemaphoreType.DMA((2 * n,)),
        ],
        compiler_params=pltpu.CompilerParams(
            collective_id=0, has_side_effects=True, vmem_limit_bytes=56 * 1024 * 1024
        ),
        cost_estimate=pl.CostEstimate(
            flops=6 * rows * width * ff, bytes_accessed=6 * width * ff, transcendentals=rows * ff
        ),
        name="expert_layer",
    )(rows_in, gate_w, up_w, down_w)

def attend_kernel(
    n_ctx, score_scale, q_nope, q_rope, kv, w_uk, w_uv, wo_hbm, out, keys, queries, heads, acc, wo,
    w_sem, kv_send, kv_recv, core_send, core_recv, h_send, h_recv,
):
    p = lax.axis_index("ctx")
    e = lax.axis_index("exp")
    last = n_ctx - 1
    half = e % 2
    sibling = e + 1 - 2 * half
    tok = q_nope.shape[0]
    part = tok // 2
    head_count, nope, lat = w_uk.shape
    vhead = w_uv.shape[2]
    rope2 = kv.shape[1] - lat
    pairs = head_count // 2
    total = keys.shape[0]

    load = pltpu.make_async_copy(wo_hbm, wo, w_sem)
    load.start()

    barrier = pltpu.get_barrier_semaphore()
    for o in range(n_ctx):

        @pl.when(p != o)
        def _():
            pl.semaphore_signal(barrier, inc=1, device_id={"ctx": o}, device_id_type=MESH)

    pl.semaphore_signal(barrier, inc=1, device_id={"exp": sibling}, device_id_type=MESH)
    pl.semaphore_wait(barrier, n_ctx)

    def kv_copy(i):
        return pltpu.make_async_remote_copy(
            src_ref=kv.at[pl.ds(pl.multiple_of(half * part, part), part)],
            dst_ref=keys.at[pl.ds(pl.multiple_of(p * tok + half * part, part), part)],
            send_sem=kv_send.at[i],
            recv_sem=kv_recv.at[p],
            device_id={"ctx": jnp.minimum(p + 1 + i, last)},
            device_id_type=MESH,
        )

    def kv_arrival(o):
        at = pl.ds(pl.multiple_of(o * tok + half * part, part), part)
        return pltpu.make_async_remote_copy(
            src_ref=keys.at[at],
            dst_ref=keys.at[at],
            send_sem=kv_send.at[0],
            recv_sem=kv_recv.at[o],
            device_id={"ctx": jnp.maximum(p - 1, 0)},
            device_id_type=MESH,
        )

    def core_copy(o, side):
        at = pl.ds(pl.multiple_of(o * tok + side * part, part), part)
        return pltpu.make_async_remote_copy(
            src_ref=keys.at[at],
            dst_ref=keys.at[at],
            send_sem=core_send.at[o],
            recv_sem=core_recv.at[o],
            device_id={"exp": sibling},
            device_id_type=MESH,
        )

    for i in range(last):

        @pl.when(p + 1 + i <= last)
        def _():
            kv_copy(i).start()

    for o in range(n_ctx):

        @pl.when(p == o)
        def _():
            keys[pl.ds(o * tok, tok), :] = kv[...]

        @pl.when(p < o)
        def _():
            keys[pl.ds(o * tok, tok), :] = jnp.zeros((tok, keys.shape[1]), keys.dtype)

    @pl.loop(0, pairs)
    def _(s):
        rope = q_rope[:, pl.ds(pl.multiple_of(s * rope2, rope2), rope2)]
        lane = lax.broadcasted_iota(jnp.int32, rope.shape, 1)
        for a in range(2):
            h = 2 * s + a
            queries[h, :, pl.ds(0, lat)] = jnp.dot(
                q_nope[:, pl.ds(pl.multiple_of(h * nope, nope), nope)],
                w_uk[h],
                preferred_element_type=jnp.float32,
            ).astype(queries.dtype)
            own = (lane < rope2 // 2) if a == 0 else (lane >= rope2 // 2)
            queries[h, :, pl.ds(lat, rope2)] = jnp.where(own, rope, jnp.zeros_like(rope))

    for o in reversed(range(last)):

        @pl.when(o < p)
        def _():
            kv_arrival(o).wait_recv()
            core_copy(o, half).start()

    for o in reversed(range(last)):

        @pl.when(o < p)
        def _():
            core_copy(o, 1 - half).wait_recv()

    def head_copy(way, o, t):
        at = pl.ds(pl.multiple_of(o * tok, tok), tok)
        cols = pl.ds(pl.multiple_of((t % 2) * 2 * vhead, 2 * vhead), 2 * vhead)
        there = jnp.minimum(p + 1, last) if way == 0 else jnp.maximum(p - 1, 0)
        return pltpu.make_async_remote_copy(
            src_ref=heads.at[t // 2, at, cols],
            dst_ref=heads.at[t // 2, at, cols],
            send_sem=h_send.at[(way * n_ctx + o) * pairs + t],
            recv_sem=h_recv.at[o * pairs + t],
            device_id={"ctx": there},
            device_id_type=MESH,
        )

    query_pos = p * tok + lax.broadcasted_iota(jnp.int32, (tok, total), 0)
    key_pos = lax.broadcasted_iota(jnp.int32, (tok, total), 1)

    @pl.loop(0, pairs + n_ctx - 2)
    def _(s):
        @pl.when(s < pairs)
        def _():
            for a in range(2):
                h = 2 * s + a
                scores = lax.dot_general(
                    queries[h],
                    keys[...],
                    (((1,), (1,)), ((), ())),
                    preferred_element_type=jnp.float32,
                )
                scores = jnp.where(key_pos <= query_pos, scores * score_scale, NEG_FILL)
                terms = jnp.exp(scores - jnp.max(scores, axis=1, keepdims=True))
                sums = jnp.sum(terms, axis=1, keepdims=True)
                mixed = jnp.dot(
                    terms.astype(jnp.bfloat16),
                    keys[:, pl.ds(0, lat)],
                    preferred_element_type=jnp.float32,
                )
                latent_out = (mixed / sums).astype(jnp.bfloat16)
                cols = pl.ds(
                    pl.multiple_of((s % 2) * 2 * vhead + a * vhead, vhead), vhead
                )
                heads[s // 2, pl.ds(pl.multiple_of(p * tok, tok), tok), cols] = jnp.dot(
                    latent_out, w_uv[h], preferred_element_type=jnp.float32
                ).astype(heads.dtype)

            @pl.when(p < last)
            def _():
                head_copy(0, p, s).start()

            @pl.when(p > 0)
            def _():
                head_copy(1, p, s).start()

        for k in range(1, n_ctx - 1):
            t = s - k

            @pl.when((t >= 0) & (t < pairs) & (p - k >= 0) & (p < last))
            def _():
                head_copy(0, p - k, t).wait_recv()
                head_copy(0, p - k, t).start()

            @pl.when((t >= 0) & (t < pairs) & (p + k <= last) & (p > 0))
            def _():
                head_copy(1, p + k, t).wait_recv()
                head_copy(1, p + k, t).start()

    load.wait()
    width = out.shape[1]
    tile = 256 if width % 256 == 0 else 128
    depth = 4 * vhead
    groups = pairs // 2
    for g in range(groups):
        for t in (2 * g, 2 * g + 1):

            @pl.when(p == last)
            def _():
                for o in range(last):
                    head_copy(0, o, t).wait_recv()

            @pl.when(p == 0)
            def _():
                for o in range(1, n_ctx):
                    head_copy(1, o, t).wait_recv()

        @pl.loop(0, width // tile)
        def _(c):
            cols = pl.ds(pl.multiple_of(c * tile, tile), tile)
            term = jnp.dot(
                heads[g], wo[pl.ds(g * depth, depth), cols], preferred_element_type=jnp.float32
            )
            if g > 0:
                term = acc[:, cols] + term
            if g < groups - 1:
                acc[:, cols] = term
            else:
                out[:, cols] = term.astype(out.dtype)

    for i in range(last):

        @pl.when(p + 1 + i <= last)
        def _():
            kv_copy(i).wait_send()

        @pl.when(i < p)
        def _():
            core_copy(i, half).wait_send()

    @pl.loop(0, pairs)
    def _(t):
        for o in range(n_ctx):

            @pl.when((o <= p) & (p < last))
            def _():
                head_copy(0, o, t).wait_send()

            @pl.when((o >= p) & (p > 0))
            def _():
                head_copy(1, o, t).wait_send()


def attend(q_nope, q_rope, kv, w_uk, w_uv, w_out, score_scale):
    n_ctx = lax.axis_size("ctx")
    tok = q_nope.shape[0]
    head_count, nope, lat = w_uk.shape
    vhead = w_uv.shape[2]
    pairs = head_count // 2
    total = n_ctx * tok
    width = w_out.shape[1]
    dma = pltpu.SemaphoreType.DMA
    return pl.pallas_call(
        partial(attend_kernel, n_ctx, score_scale),
        out_shape=jax.ShapeDtypeStruct((total, width), jnp.bfloat16),
        in_specs=[pl.BlockSpec(memory_space=pltpu.VMEM)] * 5
        + [pl.BlockSpec(memory_space=pl.ANY)],
        out_specs=pl.BlockSpec(memory_space=pltpu.VMEM),
        scratch_shapes=[
            pltpu.VMEM((total, kv.shape[1]), jnp.bfloat16),
            pltpu.VMEM((head_count, tok, kv.shape[1]), jnp.bfloat16),
            pltpu.VMEM((pairs // 2, total, 4 * vhead), jnp.bfloat16),
            pltpu.VMEM((total, width), jnp.float32),
            pltpu.VMEM(w_out.shape, jnp.bfloat16),
            dma,
            dma((n_ctx,)),
            dma((n_ctx,)),
            dma((n_ctx,)),
            dma((n_ctx,)),
            dma((2 * n_ctx * pairs,)),
            dma((n_ctx * pairs,)),
        ],
        compiler_params=pltpu.CompilerParams(
            collective_id=1, has_side_effects=True, vmem_limit_bytes=56 * 1024 * 1024
        ),
        cost_estimate=pl.CostEstimate(
            flops=2 * total * width * w_out.shape[0],
            bytes_accessed=2 * w_out.size,
            transcendentals=head_count * tok * total,
        ),
        name="attend",
    )(q_nope, q_rope, kv, w_uk, w_uv, w_out)


def exp_kernel(bits, cols, spread, *refs):
    refs = list(refs)
    mine = refs.pop(0)
    extra = refs.pop(0) if spread else None
    out = refs.pop(0)
    every = refs.pop(0) if spread else None
    sums = [[refs.pop(0) for _ in range(bits)] for _ in cols]
    came = [[refs.pop(0) for _ in range(bits)] for _ in cols]
    rs_send, rs_recv = refs.pop(0), refs.pop(0)
    if spread:
        ag_send, ag_recv = refs.pop(0), refs.pop(0)

    e = lax.axis_index("exp")
    bit = [(e // (1 << b)) % 2 for b in range(bits)]
    partner = [e + (1 - 2 * bit[b]) * (1 << b) for b in range(bits)]
    orders = [list(range(bits)), [0] + list(range(bits - 1, 0, -1))]

    barrier = pltpu.get_barrier_semaphore()
    for b in range(bits):
        pl.semaphore_signal(barrier, inc=1, device_id={"exp": partner[b]}, device_id_type=MESH)
    pl.semaphore_wait(barrier, bits)

    def place(free, at):
        return tuple(at.get(b, slice(None)) for b in free)

    top = range(bits - 1, -1, -1)
    width = mine.shape[-1]
    spot = tuple(bit[b] for b in top)
    copies = []

    def start_sum(f, j):
        start, size = cols[f]
        order = orders[f % 2]
        b = order[j]
        there = place([x for x in top if x not in order[:j]], {b: 1 - bit[b]})
        if j == 0:
            src = mine.at[there + (slice(None), pl.ds(start, size))]
        else:
            src = sums[f][j - 1].at[there]
        copy = pltpu.make_async_remote_copy(
            src_ref=src,
            dst_ref=came[f][j],
            send_sem=rs_send.at[f * bits + j],
            recv_sem=rs_recv.at[f * bits + j],
            device_id={"exp": partner[b]},
            device_id_type=MESH,
        )
        copy.start()
        copies.append(copy)
        return copy

    def finish_sum(f, j, copy):
        start, size = cols[f]
        order = orders[f % 2]
        b = order[j]
        here = place([x for x in top if x not in order[:j]], {b: bit[b]})
        copy.wait_recv()
        if j == 0:
            own = mine[here + (slice(None), pl.ds(start, size))]
        else:
            own = sums[f][j - 1][here]
        sums[f][j][...] = (
            own.astype(jnp.float32) + came[f][j][...].astype(jnp.float32)
        ).astype(jnp.bfloat16)

    def start_spread(f, j):
        start, size = cols[f]
        order = orders[f % 2]
        if f == len(cols) - 1:
            size = size + extra.shape[-1]
        at = place(top, {b: bit[b] for b in order[: j + 1]})
        block = every.at[at + (slice(None), pl.ds(start, size))]
        copy = pltpu.make_async_remote_copy(
            src_ref=block,
            dst_ref=block,
            send_sem=ag_send.at[f * bits + j],
            recv_sem=ag_recv.at[f * bits + j],
            device_id={"exp": partner[order[j]]},
            device_id_type=MESH,
        )
        copy.start()
        copies.append(copy)
        return copy

    if spread:
        every[spot + (slice(None), pl.ds(width, extra.shape[-1]))] = extra[...]
    flying = [start_sum(f, 0) for f in range(len(cols))]
    for j in range(bits):
        for f, (start, size) in enumerate(cols):
            finish_sum(f, j, flying[f])
            if j < bits - 1:
                flying[f] = start_sum(f, j + 1)
            else:
                if spread:
                    every[spot + (slice(None), pl.ds(start, size))] = sums[f][j][...]
                    flying[f] = start_spread(f, j)
                out[:, pl.ds(start, size)] = sums[f][j][...]
    if spread:
        for j in reversed(range(bits)):
            for f in range(len(cols)):
                flying[f].wait_recv()
                if j > 0:
                    flying[f] = start_spread(f, j - 1)
    for copy in copies:
        copy.wait_send()


def exp_sum(rows_in, extra, collective_id):
    n_exp = lax.axis_size("exp")
    bits = n_exp.bit_length() - 1
    total, width = rows_in.shape
    rows = total // n_exp
    spread = extra is not None
    lanes = width // 128
    sizes = [128 * ((lanes + 3 - f) // 4) for f in range(4)]
    cols = tuple((sum(sizes[:f]), sizes[f]) for f in range(4))
    vmem = pl.BlockSpec(memory_space=pltpu.VMEM)
    shapes = []
    for _ in range(2):
        for _, size in cols:
            for j in range(bits):
                shapes.append(pltpu.VMEM((2,) * (bits - 1 - j) + (rows, size), jnp.bfloat16))
    shapes += [pltpu.SemaphoreType.DMA((4 * bits,))] * (4 if spread else 2)
    out_shape = [jax.ShapeDtypeStruct((rows, width), jnp.bfloat16)]
    operands = [rows_in.reshape((2,) * bits + (rows, width))]
    if spread:
        wide = width + extra.shape[1]
        out_shape.append(jax.ShapeDtypeStruct((2,) * bits + (rows, wide), jnp.bfloat16))
        operands.append(extra)
    got = pl.pallas_call(
        partial(exp_kernel, bits, cols, spread),
        out_shape=out_shape,
        in_specs=[vmem] * len(operands),
        out_specs=[vmem] * len(out_shape),
        scratch_shapes=shapes,
        compiler_params=pltpu.CompilerParams(
            collective_id=collective_id, has_side_effects=True, vmem_limit_bytes=40 * 1024 * 1024
        ),
        cost_estimate=pl.CostEstimate(
            flops=2 * total * width, bytes_accessed=4 * total * width, transcendentals=0
        ),
        name="exp_sum_spread" if spread else "exp_sum",
    )(*operands)
    if spread:
        return got[0], got[1].reshape(total, wide)
    return got[0]


def local(
    q_nope,
    q_rope,
    kv_latent,
    key_rope,
    w_uk,
    w_uv,
    w_out,
    w_gate,
    w_up,
    w_down,
    route_ids,
    route_gates,
):
    nope_size = w_uk.shape[1]
    rope_size = key_rope.shape[1]
    n_exp = lax.axis_size("exp")
    keys = jnp.concatenate([kv_latent, key_rope, key_rope], axis=1)
    partial_out = attend(
        q_nope, q_rope, keys, w_uk, w_uv, w_out, 1.0 / math.sqrt(nope_size + rope_size)
    )
    out_rows, top_count = route_ids.shape
    routing = jnp.concatenate([route_ids.astype(jnp.bfloat16), route_gates], axis=1)
    routing = jnp.pad(routing, ((0, 0), (0, 128 - 2 * top_count)))
    attn_out, gathered = exp_sum(partial_out, routing, 2)
    total, width = partial_out.shape
    capacity = 3 * out_rows * top_count // (2 * n_exp)
    slot_total = n_exp * capacity
    ids = gathered[:, width : width + top_count].astype(jnp.float32)
    gates = gathered[:, width + top_count : width + 2 * top_count].astype(jnp.float32)
    named = ids == lax.axis_index("exp").astype(jnp.float32)
    chosen = jnp.any(named, axis=1)
    gate = jnp.sum(jnp.where(named, gates, 0.0), axis=1)
    below = jnp.tril(jnp.ones((out_rows, out_rows), jnp.bfloat16), -1)
    ranks = lax.dot_general(
        chosen.astype(jnp.bfloat16).reshape(n_exp, out_rows),
        below,
        (((1,), (1,)), ((), ())),
        preferred_element_type=jnp.float32,
    ).astype(jnp.int32)
    slots = ranks + capacity * jnp.arange(n_exp, dtype=jnp.int32)[:, None]
    slots = jnp.where(chosen, slots.reshape(total), -1)
    slot_range = jnp.arange(slot_total, dtype=jnp.int32)
    placing = (slots[None, :] == slot_range[:, None]).astype(jnp.bfloat16)
    arrived = jnp.dot(
        placing, gathered[:, :width], preferred_element_type=jnp.float32
    ).astype(jnp.bfloat16)
    expert_out = expert_layer(arrived, w_gate[0], w_up[0], w_down[0])
    weighting = jnp.where(slots[:, None] == slot_range[None, :], gate[:, None], 0.0)
    share = jnp.dot(
        weighting.astype(jnp.bfloat16), expert_out, preferred_element_type=jnp.float32
    ).astype(jnp.bfloat16)
    return (attn_out, exp_sum(share, None, 3))


def solution(mesh):
    placed = (
        P("ctx", "exp"),
        P("ctx", "exp"),
        P("ctx", None),
        P("ctx", None),
        P("exp", None, None),
        P("exp", None, None),
        P("exp", "ctx"),
        P("exp", "ctx", None),
        P("exp", "ctx", None),
        P("exp", None, "ctx"),
        P("exp", None),
        P("exp", None),
    )
    return jax.shard_map(
        local,
        mesh=mesh,
        in_specs=placed,
        out_specs=(P("exp", "ctx"), P("exp", "ctx")),
        check_vma=False,
    )
```

```python
from functools import partial
import math

import jax
import jax.numpy as jnp
from jax import lax
from jax.experimental import pallas as pl
from jax.experimental.pallas import tpu as pltpu
from jax.sharding import PartitionSpec as P

NEG_FILL = -1e30
MESH = pl.DeviceIdType.MESH
CHUNK = 16
SLACK = 2
AHEAD = 3


def expert_kernel(
    n_ctx, cap, slots, gates, x, wg_hbm, wu_hbm, wd_hbm, out, wg, wu, wd, picked, part, held, hid,
    w_sem, rs_send, rs_recv, ag_send, ag_recv,
):
    p = lax.axis_index("ctx")
    last = n_ctx - 1
    sources, toks = slots.shape
    rows = sources * cap
    half = rows // 2
    width, ff = wg.shape
    n = half // CHUNK
    per = cap // CHUNK
    blocks = sources // 2
    tile = 512 if ff % 512 == 0 else ff

    tiles = ff // tile
    loads = []
    for c in range(tiles):
        cols = pl.ds(c * tile, tile)
        for src, dst in ((wg_hbm, wg), (wu_hbm, wu)):
            loads.append(
                pltpu.make_async_copy(src.at[:, cols], dst.at[:, cols], w_sem.at[len(loads)])
            )
    loads.append(pltpu.make_async_copy(wd_hbm, wd, w_sem.at[len(loads)]))
    for load in loads:
        load.start()

    barrier = pltpu.get_barrier_semaphore()

    @pl.when(p > 0)
    def _():
        pl.semaphore_signal(barrier, inc=1, device_id={"ctx": p - 1}, device_id_type=MESH)

    @pl.when(p < last)
    def _():
        pl.semaphore_signal(barrier, inc=1, device_id={"ctx": p + 1}, device_id_type=MESH)

    pl.semaphore_wait(barrier, (p > 0).astype(jnp.int32) + (p < last).astype(jnp.int32))

    ahead = (jnp.minimum(p + 1, last), jnp.maximum(p - 1, 0))

    def chunk_rows(d, t):
        return pl.ds(pl.multiple_of(d * half + t * CHUNK, CHUNK), CHUNK)

    def rs_copy(d, t, src):
        at = chunk_rows(d, t)
        return pltpu.make_async_remote_copy(
            src_ref=src.at[at],
            dst_ref=held.at[at],
            send_sem=rs_send.at[d * n + t],
            recv_sem=rs_recv.at[d * n + t],
            device_id={"ctx": ahead[d]},
            device_id_type=MESH,
        )

    def ag_copy(d, t):
        at = chunk_rows(d, t)
        return pltpu.make_async_remote_copy(
            src_ref=hid.at[at],
            dst_ref=hid.at[at],
            send_sem=ag_send.at[d * n + t],
            recv_sem=ag_recv.at[d * n + t],
            device_id={"ctx": ahead[1 - d]},
            device_id_type=MESH,
        )

    def placing(b):
        slot = lax.broadcasted_iota(jnp.int32, (cap, toks), 0)
        return jnp.where(slots[pl.ds(b, 1), :] == slot, 1.0, 0.0).astype(jnp.bfloat16)

    def pick(d, block):
        b = d * blocks + block
        tokens = x[pl.ds(pl.multiple_of(b * toks, toks), toks), pl.ds(0, width)]
        picked[...] = jnp.dot(
            placing(b), tokens, preferred_element_type=jnp.float32
        ).astype(picked.dtype)

    def gate_up_tile(d, block, c):
        at = pl.ds(pl.multiple_of(d * half + block * cap, CHUNK), cap)
        base = pl.multiple_of(c * tile, tile)
        above = pl.multiple_of(ff + c * tile, tile)
        part[at, pl.ds(base, tile)] = jnp.dot(
            picked[...], wg[:, pl.ds(base, tile)], preferred_element_type=jnp.float32
        ).astype(part.dtype)
        part[at, pl.ds(above, tile)] = jnp.dot(
            picked[...], wu[:, pl.ds(base, tile)], preferred_element_type=jnp.float32
        ).astype(part.dtype)

    def gate_up(d, block):
        pick(d, block)

        @pl.loop(0, tiles)
        def _(c):
            gate_up_tile(d, block, c)

    down_tile = 256 if width % 256 == 0 else 128

    def down(d, block):
        b = d * blocks + block
        at = pl.ds(pl.multiple_of(d * half + block * cap, CHUNK), cap)
        to = pl.ds(pl.multiple_of(b * toks, toks), toks)
        place = placing(b)
        gate = gates[to, :]

        @pl.loop(0, width // down_tile)
        def _(c):
            cols = pl.ds(pl.multiple_of(c * down_tile, down_tile), down_tile)
            expert_out = jnp.dot(
                hid[at, :], wd[:, cols], preferred_element_type=jnp.float32
            ).astype(jnp.bfloat16)
            own = lax.dot_general(
                place, expert_out, (((0,), (0,)), ((), ())), preferred_element_type=jnp.float32
            )
            out[to, cols] = (own * gate).astype(out.dtype)

    first = (2 * p > last).astype(jnp.int32)
    pick(first, 0)
    for c in range(tiles):
        loads[2 * c].wait()
        loads[2 * c + 1].wait()
        gate_up_tile(first, 0, c)

    @pl.loop(0, n + 2 * last * SLACK)
    def _(s):
        for d in range(2):
            k = p if d == 0 else last - p
            t = s - k * SLACK

            @pl.when((t >= 0) & (t < n))
            def _():
                at = chunk_rows(d, t)

                @pl.when((k == 0) & (t >= AHEAD))
                def _():
                    rs_copy(d, t - AHEAD, part).wait_send()

                @pl.when(k == 0)
                def _():
                    rs_copy(d, t, part).start()

                @pl.when((k > 0) & (k < last))
                def _():
                    rs_copy(d, t, held).wait_recv()
                    held[at, :] = (
                        held[at, :].astype(jnp.float32) + part[at, :].astype(jnp.float32)
                    ).astype(held.dtype)
                    rs_copy(d, t, held).start()

                @pl.when(k == last)
                def _():
                    rs_copy(d, t, held).wait_recv()
                    gate = held[at, pl.ds(0, ff)].astype(jnp.float32) + part[
                        at, pl.ds(0, ff)
                    ].astype(jnp.float32)
                    up = held[at, pl.ds(ff, ff)].astype(jnp.float32) + part[
                        at, pl.ds(ff, ff)
                    ].astype(jnp.float32)
                    hid[at, :] = (gate / (1.0 + jnp.exp(-gate)) * up).astype(hid.dtype)
                    ag_copy(d, t).start()

        for d in range(2):
            j = last - p if d == 0 else p
            u = s - (last + j) * SLACK

            @pl.when((u >= 0) & (u < n))
            def _():
                @pl.when(j > 0)
                def _():
                    ag_copy(d, u).wait_recv()

                    @pl.when(j < last)
                    def _():
                        ag_copy(d, u).start()

        i = s + 1

        @pl.when(i < 2 * blocks)
        def _():
            gate_up((i + first) % 2, i // 2)

        @pl.when(s == last)
        def _():
            loads[-1].wait()

        for d in range(2):
            j = last - p if d == 0 else p
            u = s - (last + j) * SLACK

            @pl.when((u >= 0) & (u < n) & (u % per == per - 1))
            def _():
                down(d, u // per)

    @pl.loop(0, n)
    def _(t):
        for d in range(2):
            k = p if d == 0 else last - p

            @pl.when((k < last) & ((k > 0) | (t >= n - AHEAD)))
            def _():
                rs_copy(d, t, held).wait_send()

            @pl.when(k > 0)
            def _():
                ag_copy(d, t).wait_send()


def expert_layer(slots, gates, tokens, gate_w, up_w, down_w, cap):
    n_ctx = lax.axis_size("ctx")
    width, ff = gate_w.shape
    rows = slots.shape[0] * cap
    n = rows // 2 // CHUNK
    return pl.pallas_call(
        partial(expert_kernel, n_ctx, cap),
        out_shape=jax.ShapeDtypeStruct((slots.size, width), jnp.bfloat16),
        in_specs=[pl.BlockSpec(memory_space=pltpu.VMEM)] * 3
        + [pl.BlockSpec(memory_space=pl.ANY)] * 3,
        out_specs=pl.BlockSpec(memory_space=pltpu.VMEM),
        scratch_shapes=[
            pltpu.VMEM((width, ff), jnp.bfloat16),
            pltpu.VMEM((width, ff), jnp.bfloat16),
            pltpu.VMEM((ff, width), jnp.bfloat16),
            pltpu.VMEM((cap, width), jnp.bfloat16),
            pltpu.VMEM((rows, 2 * ff), jnp.bfloat16),
            pltpu.VMEM((rows, 2 * ff), jnp.bfloat16),
            pltpu.VMEM((rows, ff), jnp.bfloat16),
            pltpu.SemaphoreType.DMA((2 * max(1, ff // 512) + 1,)),
            pltpu.SemaphoreType.DMA((2 * n,)),
            pltpu.SemaphoreType.DMA((2 * n,)),
            pltpu.SemaphoreType.DMA((2 * n,)),
            pltpu.SemaphoreType.DMA((2 * n,)),
        ],
        compiler_params=pltpu.CompilerParams(
            collective_id=0, has_side_effects=True, vmem_limit_bytes=56 * 1024 * 1024
        ),
        cost_estimate=pl.CostEstimate(
            flops=6 * rows * width * ff, bytes_accessed=6 * width * ff, transcendentals=rows * ff
        ),
        name="expert_layer",
    )(slots, gates, tokens, gate_w, up_w, down_w)


def attend_kernel(
    n_ctx, score_scale, q_nope, q_rope, kv, w_uk, w_uv, wo_hbm, out, keys, queries, heads, acc, wo,
    w_sem, kv_send, kv_recv, core_send, core_recv, h_send, h_recv,
):
    p = lax.axis_index("ctx")
    e = lax.axis_index("exp")
    last = n_ctx - 1
    half = e % 2
    sibling = e + 1 - 2 * half
    tok = q_nope.shape[0]
    part = tok // 2
    head_count, nope, lat = w_uk.shape
    vhead = w_uv.shape[2]
    rope2 = kv.shape[1] - lat
    pairs = head_count // 2
    total = keys.shape[0]

    load = pltpu.make_async_copy(wo_hbm, wo, w_sem)
    load.start()

    barrier = pltpu.get_barrier_semaphore()
    for o in range(n_ctx):

        @pl.when(p != o)
        def _():
            pl.semaphore_signal(barrier, inc=1, device_id={"ctx": o}, device_id_type=MESH)

    pl.semaphore_signal(barrier, inc=1, device_id={"exp": sibling}, device_id_type=MESH)
    pl.semaphore_wait(barrier, n_ctx)

    def kv_copy(i):
        return pltpu.make_async_remote_copy(
            src_ref=kv.at[pl.ds(pl.multiple_of(half * part, part), part)],
            dst_ref=keys.at[pl.ds(pl.multiple_of(p * tok + half * part, part), part)],
            send_sem=kv_send.at[i],
            recv_sem=kv_recv.at[p],
            device_id={"ctx": jnp.minimum(p + 1 + i, last)},
            device_id_type=MESH,
        )

    def kv_arrival(o):
        at = pl.ds(pl.multiple_of(o * tok + half * part, part), part)
        return pltpu.make_async_remote_copy(
            src_ref=keys.at[at],
            dst_ref=keys.at[at],
            send_sem=kv_send.at[0],
            recv_sem=kv_recv.at[o],
            device_id={"ctx": jnp.maximum(p - 1, 0)},
            device_id_type=MESH,
        )

    def core_copy(o, side):
        at = pl.ds(pl.multiple_of(o * tok + side * part, part), part)
        return pltpu.make_async_remote_copy(
            src_ref=keys.at[at],
            dst_ref=keys.at[at],
            send_sem=core_send.at[o],
            recv_sem=core_recv.at[o],
            device_id={"exp": sibling},
            device_id_type=MESH,
        )

    for i in range(last):

        @pl.when(p + 1 + i <= last)
        def _():
            kv_copy(i).start()

    for o in range(n_ctx):

        @pl.when(p == o)
        def _():
            keys[pl.ds(o * tok, tok), :] = kv[...]

        @pl.when(p < o)
        def _():
            keys[pl.ds(o * tok, tok), :] = jnp.zeros((tok, keys.shape[1]), keys.dtype)

    @pl.loop(0, pairs)
    def _(s):
        rope = q_rope[:, pl.ds(pl.multiple_of(s * rope2, rope2), rope2)]
        lane = lax.broadcasted_iota(jnp.int32, rope.shape, 1)
        for a in range(2):
            h = 2 * s + a
            queries[h, :, pl.ds(0, lat)] = jnp.dot(
                q_nope[:, pl.ds(pl.multiple_of(h * nope, nope), nope)],
                w_uk[h],
                preferred_element_type=jnp.float32,
            ).astype(queries.dtype)
            own = (lane < rope2 // 2) if a == 0 else (lane >= rope2 // 2)
            queries[h, :, pl.ds(lat, rope2)] = jnp.where(own, rope, jnp.zeros_like(rope))

    for o in reversed(range(last)):

        @pl.when(o < p)
        def _():
            kv_arrival(o).wait_recv()
            core_copy(o, half).start()

    for o in reversed(range(last)):

        @pl.when(o < p)
        def _():
            core_copy(o, 1 - half).wait_recv()

    def head_copy(way, o, t):
        at = pl.ds(pl.multiple_of(o * tok, tok), tok)
        cols = pl.ds(pl.multiple_of((t % 2) * 2 * vhead, 2 * vhead), 2 * vhead)
        there = jnp.minimum(p + 1, last) if way == 0 else jnp.maximum(p - 1, 0)
        return pltpu.make_async_remote_copy(
            src_ref=heads.at[t // 2, at, cols],
            dst_ref=heads.at[t // 2, at, cols],
            send_sem=h_send.at[(way * n_ctx + o) * pairs + t],
            recv_sem=h_recv.at[o * pairs + t],
            device_id={"ctx": there},
            device_id_type=MESH,
        )

    query_pos = p * tok + lax.broadcasted_iota(jnp.int32, (tok, total), 0)
    key_pos = lax.broadcasted_iota(jnp.int32, (tok, total), 1)

    @pl.loop(0, pairs + n_ctx - 2)
    def _(s):
        @pl.when(s < pairs)
        def _():
            for a in range(2):
                h = 2 * s + a
                scores = lax.dot_general(
                    queries[h],
                    keys[...],
                    (((1,), (1,)), ((), ())),
                    preferred_element_type=jnp.float32,
                )
                scores = jnp.where(key_pos <= query_pos, scores * score_scale, NEG_FILL)
                terms = jnp.exp(scores - jnp.max(scores, axis=1, keepdims=True))
                sums = jnp.sum(terms, axis=1, keepdims=True)
                mixed = jnp.dot(
                    terms.astype(jnp.bfloat16),
                    keys[:, pl.ds(0, lat)],
                    preferred_element_type=jnp.float32,
                )
                latent_out = (mixed / sums).astype(jnp.bfloat16)
                cols = pl.ds(
                    pl.multiple_of((s % 2) * 2 * vhead + a * vhead, vhead), vhead
                )
                heads[s // 2, pl.ds(pl.multiple_of(p * tok, tok), tok), cols] = jnp.dot(
                    latent_out, w_uv[h], preferred_element_type=jnp.float32
                ).astype(heads.dtype)

            @pl.when(p < last)
            def _():
                head_copy(0, p, s).start()

            @pl.when(p > 0)
            def _():
                head_copy(1, p, s).start()

        for k in range(1, n_ctx - 1):
            t = s - k

            @pl.when((t >= 0) & (t < pairs) & (p - k >= 0) & (p < last))
            def _():
                head_copy(0, p - k, t).wait_recv()
                head_copy(0, p - k, t).start()

            @pl.when((t >= 0) & (t < pairs) & (p + k <= last) & (p > 0))
            def _():
                head_copy(1, p + k, t).wait_recv()
                head_copy(1, p + k, t).start()

    load.wait()
    width = out.shape[1]
    tile = 256 if width % 256 == 0 else 128
    depth = 4 * vhead
    groups = pairs // 2
    for g in range(groups):
        for t in (2 * g, 2 * g + 1):

            @pl.when(p == last)
            def _():
                for o in range(last):
                    head_copy(0, o, t).wait_recv()

            @pl.when(p == 0)
            def _():
                for o in range(1, n_ctx):
                    head_copy(1, o, t).wait_recv()

        @pl.loop(0, width // tile)
        def _(c):
            cols = pl.ds(pl.multiple_of(c * tile, tile), tile)
            term = jnp.dot(
                heads[g], wo[pl.ds(g * depth, depth), cols], preferred_element_type=jnp.float32
            )
            if g > 0:
                term = acc[:, cols] + term
            if g < groups - 1:
                acc[:, cols] = term
            else:
                out[:, cols] = term.astype(out.dtype)

    for i in range(last):

        @pl.when(p + 1 + i <= last)
        def _():
            kv_copy(i).wait_send()

        @pl.when(i < p)
        def _():
            core_copy(i, half).wait_send()

    @pl.loop(0, pairs)
    def _(t):
        for o in range(n_ctx):

            @pl.when((o <= p) & (p < last))
            def _():
                head_copy(0, o, t).wait_send()

            @pl.when((o >= p) & (p > 0))
            def _():
                head_copy(1, o, t).wait_send()


def attend(q_nope, q_rope, kv, w_uk, w_uv, w_out, score_scale):
    n_ctx = lax.axis_size("ctx")
    tok = q_nope.shape[0]
    head_count, nope, lat = w_uk.shape
    vhead = w_uv.shape[2]
    pairs = head_count // 2
    total = n_ctx * tok
    width = w_out.shape[1]
    dma = pltpu.SemaphoreType.DMA
    return pl.pallas_call(
        partial(attend_kernel, n_ctx, score_scale),
        out_shape=jax.ShapeDtypeStruct((total, width), jnp.bfloat16),
        in_specs=[pl.BlockSpec(memory_space=pltpu.VMEM)] * 5
        + [pl.BlockSpec(memory_space=pl.ANY)],
        out_specs=pl.BlockSpec(memory_space=pltpu.VMEM),
        scratch_shapes=[
            pltpu.VMEM((total, kv.shape[1]), jnp.bfloat16),
            pltpu.VMEM((head_count, tok, kv.shape[1]), jnp.bfloat16),
            pltpu.VMEM((pairs // 2, total, 4 * vhead), jnp.bfloat16),
            pltpu.VMEM((total, width), jnp.float32),
            pltpu.VMEM(w_out.shape, jnp.bfloat16),
            dma,
            dma((n_ctx,)),
            dma((n_ctx,)),
            dma((n_ctx,)),
            dma((n_ctx,)),
            dma((2 * n_ctx * pairs,)),
            dma((n_ctx * pairs,)),
        ],
        compiler_params=pltpu.CompilerParams(
            collective_id=1, has_side_effects=True, vmem_limit_bytes=56 * 1024 * 1024
        ),
        cost_estimate=pl.CostEstimate(
            flops=2 * total * width * w_out.shape[0],
            bytes_accessed=2 * w_out.size,
            transcendentals=head_count * tok * total,
        ),
        name="attend",
    )(q_nope, q_rope, kv, w_uk, w_uv, w_out)


def exp_kernel(bits, cols, spread, *refs):
    refs = list(refs)
    mine = refs.pop(0)
    extra = refs.pop(0) if spread else None
    out = refs.pop(0)
    every = refs.pop(0) if spread else None
    sums = [[refs.pop(0) for _ in range(bits)] for _ in cols]
    came = [[refs.pop(0) for _ in range(bits)] for _ in cols]
    rs_send, rs_recv = refs.pop(0), refs.pop(0)
    if spread:
        ag_send, ag_recv = refs.pop(0), refs.pop(0)

    e = lax.axis_index("exp")
    bit = [(e // (1 << b)) % 2 for b in range(bits)]
    partner = [e + (1 - 2 * bit[b]) * (1 << b) for b in range(bits)]
    orders = [list(range(bits)), [0] + list(range(bits - 1, 0, -1))]

    barrier = pltpu.get_barrier_semaphore()
    for b in range(bits):
        pl.semaphore_signal(barrier, inc=1, device_id={"exp": partner[b]}, device_id_type=MESH)
    pl.semaphore_wait(barrier, bits)

    def place(free, at):
        return tuple(at.get(b, slice(None)) for b in free)

    top = range(bits - 1, -1, -1)
    width = mine.shape[-1]
    spot = tuple(bit[b] for b in top)
    copies = []

    def start_sum(f, j):
        start, size = cols[f]
        order = orders[f % 2]
        b = order[j]
        there = place([x for x in top if x not in order[:j]], {b: 1 - bit[b]})
        if j == 0:
            src = mine.at[there + (slice(None), pl.ds(start, size))]
        else:
            src = sums[f][j - 1].at[there]
        copy = pltpu.make_async_remote_copy(
            src_ref=src,
            dst_ref=came[f][j],
            send_sem=rs_send.at[f * bits + j],
            recv_sem=rs_recv.at[f * bits + j],
            device_id={"exp": partner[b]},
            device_id_type=MESH,
        )
        copy.start()
        copies.append(copy)
        return copy

    def finish_sum(f, j, copy):
        start, size = cols[f]
        order = orders[f % 2]
        b = order[j]
        here = place([x for x in top if x not in order[:j]], {b: bit[b]})
        copy.wait_recv()
        if j == 0:
            own = mine[here + (slice(None), pl.ds(start, size))]
        else:
            own = sums[f][j - 1][here]
        sums[f][j][...] = (
            own.astype(jnp.float32) + came[f][j][...].astype(jnp.float32)
        ).astype(jnp.bfloat16)

    def start_spread(f, j):
        start, size = cols[f]
        order = orders[f % 2]
        if f == len(cols) - 1:
            size = size + extra.shape[-1]
        at = place(top, {b: bit[b] for b in order[: j + 1]})
        block = every.at[at + (slice(None), pl.ds(start, size))]
        copy = pltpu.make_async_remote_copy(
            src_ref=block,
            dst_ref=block,
            send_sem=ag_send.at[f * bits + j],
            recv_sem=ag_recv.at[f * bits + j],
            device_id={"exp": partner[order[j]]},
            device_id_type=MESH,
        )
        copy.start()
        copies.append(copy)
        return copy

    if spread:
        every[spot + (slice(None), pl.ds(width, extra.shape[-1]))] = extra[...]
    flying = [start_sum(f, 0) for f in range(len(cols))]
    for j in range(bits):
        for f, (start, size) in enumerate(cols):
            finish_sum(f, j, flying[f])
            if j < bits - 1:
                flying[f] = start_sum(f, j + 1)
            else:
                if spread:
                    every[spot + (slice(None), pl.ds(start, size))] = sums[f][j][...]
                    flying[f] = start_spread(f, j)
                out[:, pl.ds(start, size)] = sums[f][j][...]
    if spread:
        for j in reversed(range(bits)):
            for f in range(len(cols)):
                flying[f].wait_recv()
                if j > 0:
                    flying[f] = start_spread(f, j - 1)
    for copy in copies:
        copy.wait_send()


def exp_sum(rows_in, extra, collective_id):
    n_exp = lax.axis_size("exp")
    bits = n_exp.bit_length() - 1
    total, width = rows_in.shape
    rows = total // n_exp
    spread = extra is not None
    lanes = width // 128
    sizes = [128 * ((lanes + 3 - f) // 4) for f in range(4)]
    cols = tuple((sum(sizes[:f]), sizes[f]) for f in range(4))
    vmem = pl.BlockSpec(memory_space=pltpu.VMEM)
    shapes = []
    for _ in range(2):
        for _, size in cols:
            for j in range(bits):
                shapes.append(pltpu.VMEM((2,) * (bits - 1 - j) + (rows, size), jnp.bfloat16))
    shapes += [pltpu.SemaphoreType.DMA((4 * bits,))] * (4 if spread else 2)
    out_shape = [jax.ShapeDtypeStruct((rows, width), jnp.bfloat16)]
    operands = [rows_in.reshape((2,) * bits + (rows, width))]
    if spread:
        wide = width + extra.shape[1]
        out_shape.append(jax.ShapeDtypeStruct((2,) * bits + (rows, wide), jnp.bfloat16))
        operands.append(extra)
    got = pl.pallas_call(
        partial(exp_kernel, bits, cols, spread),
        out_shape=out_shape,
        in_specs=[vmem] * len(operands),
        out_specs=[vmem] * len(out_shape),
        scratch_shapes=shapes,
        compiler_params=pltpu.CompilerParams(
            collective_id=collective_id, has_side_effects=True, vmem_limit_bytes=40 * 1024 * 1024
        ),
        cost_estimate=pl.CostEstimate(
            flops=2 * total * width, bytes_accessed=4 * total * width, transcendentals=0
        ),
        name="exp_sum_spread" if spread else "exp_sum",
    )(*operands)
    if spread:
        return got[0], got[1].reshape(total, wide)
    return got[0]


def local(
    q_nope,
    q_rope,
    kv_latent,
    key_rope,
    w_uk,
    w_uv,
    w_out,
    w_gate,
    w_up,
    w_down,
    route_ids,
    route_gates,
):
    nope_size = w_uk.shape[1]
    rope_size = key_rope.shape[1]
    n_exp = lax.axis_size("exp")
    keys = jnp.concatenate([kv_latent, key_rope, key_rope], axis=1)
    partial_out = attend(
        q_nope, q_rope, keys, w_uk, w_uv, w_out, 1.0 / math.sqrt(nope_size + rope_size)
    )
    out_rows, top_count = route_ids.shape
    routing = jnp.concatenate([route_ids.astype(jnp.bfloat16), route_gates], axis=1)
    routing = jnp.pad(routing, ((0, 0), (0, 128 - 2 * top_count)))
    attn_out, gathered = exp_sum(partial_out, routing, 2)
    total, width = partial_out.shape
    capacity = 3 * out_rows * top_count // (2 * n_exp)
    ids = gathered[:, width : width + top_count].astype(jnp.float32)
    gates = gathered[:, width + top_count : width + 2 * top_count].astype(jnp.float32)
    named = ids == lax.axis_index("exp").astype(jnp.float32)
    chosen = jnp.any(named, axis=1)
    gate = jnp.sum(jnp.where(named, gates, 0.0), axis=1)
    below = jnp.tril(jnp.ones((out_rows, out_rows), jnp.bfloat16), -1)
    ranks = lax.dot_general(
        chosen.astype(jnp.bfloat16).reshape(n_exp, out_rows),
        below,
        (((1,), (1,)), ((), ())),
        preferred_element_type=jnp.float32,
    ).astype(jnp.int32)
    slots = jnp.where(chosen.reshape(n_exp, out_rows), ranks, -1)
    share = expert_layer(slots, gate[:, None], gathered, w_gate[0], w_up[0], w_down[0], capacity)
    return (attn_out, exp_sum(share, None, 3))


def solution(mesh):
    placed = (
        P("ctx", "exp"),
        P("ctx", "exp"),
        P("ctx", None),
        P("ctx", None),
        P("exp", None, None),
        P("exp", None, None),
        P("exp", "ctx"),
        P("exp", "ctx", None),
        P("exp", "ctx", None),
        P("exp", None, "ctx"),
        P("exp", None),
        P("exp", None),
    )
    return jax.shard_map(
        local,
        mesh=mesh,
        in_specs=placed,
        out_specs=(P("exp", "ctx"), P("exp", "ctx")),
        check_vma=False,
    )
```
